32 devices in a mesh: gx: 4 (over y, core), gy: 2 (over x), gz: 4 (over z).
Axes of the slice: x: 2, y: 2, z: 4, core: 2. Of those that a mesh axis runs over, the one named last changes fastest.
Arguments:
- fields: float32 [6, 16, 64, 256], P(None, 'gz', 'gx', 'gy'), may hold values from -6 to 6
- material: int32 [16, 64, 256], P('gz', 'gx', 'gy'), may hold values from 0 to 15
- faces: int32 [3, 16, 64, 256], P(None, 'gz', 'gx', 'gy'), may hold values 0 or 1
- permittivity: float32 [16], replicated, may hold values from 1 to 8
- losses: float32 [16], replicated, may hold values from 0.02 to 1
- angles: float32 [2, 512], replicated, may hold values from -3.140625 to 3.140625
- wavenumbers: float32 [4], replicated, may hold values from 0.2 to 1.6
Outputs:
- fields_next: float32 [6, 16, 64, 256], P(None, 'gz', 'gx', 'gy')
- far_field: float32 [512, 96], P(('gx', 'gy', 'gz'))
The draws below stay inside these ranges and needn't reach their ends.
Inputs may be any that keep to these rules, and one draw needn't show every extreme that they name: material indices into the tables. `faces`: 1 where a cell lies on the face of that normal, else 0.
All inputs are finite; a program needn't handle non-finite values. No bound on the sum of `faces` on one device may be relied on, other than what follows from the above.
Results may differ from the reference program's by a relative error of at most 0.0038.
Values may be sent and summed in bfloat16 or wider, within the bound.
A program may use at most 64 MiB of HBM per device.

```python
import math
import jax
import jax.numpy as jnp
from jax import lax

CX = 16
CY = 128
DIR_DEV = 16
NF = 4
NMAT = 16
NX = 64
NY = 256
NZ = 16
DIRS = 512
N_GX = 4
N_GY = 2


def with_ends(array, own_key, least, top_value):
    spot = [jax.random.randint(jax.random.fold_in(own_key, axis), (), 0, length) for axis, length in enumerate(array.shape)]
    longest = array.shape.index(max(array.shape))
    next_to = spot[:longest] + [(spot[longest] + 1) % array.shape[longest]] + spot[longest + 1:]
    return array.at[tuple(spot)].set(least).at[tuple(next_to)].set(top_value)


def shard_levels(own_key, shape, split, least, top_value):
    def one(axis_at, blocks):
        steps = jax.random.uniform(jax.random.fold_in(jax.random.fold_in(own_key, 6), axis_at), (blocks,), jnp.float32, least / len(split), top_value / len(split))
        return jnp.repeat(jnp.exp(steps), shape[axis_at] // blocks).reshape((-1,) + (1,) * (len(shape) - axis_at - 1))

    level = one(*split[0])
    for cut in split[1:]:
        level = level * one(*cut)
    return level


def bell_draw(key, shape, spread, most, split=(), kind=jnp.bfloat16):
    array = spread * jax.random.normal(key, shape, jnp.float32)
    if split:
        array = array * shard_levels(key, shape, split, -0.22, 0.18)
    return jnp.clip(array, -most, most).astype(kind)


def setup_inputs(seed: int = 0) -> dict:
    streams_of = jax.random.split(jax.random.key(seed), 8)
    fields = bell_draw(streams_of[0], (6, NZ, NX, NY), 1.0, 6.0, ((1, 4), (2, 4), (3, 2)), jnp.float32)
    material = with_ends(jax.random.randint(streams_of[1], (NZ, NX, NY), 0, NMAT), jax.random.fold_in(streams_of[1], 1), 0, NMAT - 1).astype(jnp.int32)
    faces = with_ends((jax.random.randint(streams_of[2], (3, NZ, NX, NY), 0, 2) < 1).astype(jnp.int32), jax.random.fold_in(streams_of[2], 1), 0, 1)
    permittivity = jnp.clip(jnp.exp(jax.random.uniform(streams_of[3], (NMAT,), jnp.float32, math.log(1.0), math.log(8.0))), 1.0, 8.0)
    losses = jnp.clip(jnp.exp(jax.random.uniform(streams_of[4], (NMAT,), jnp.float32, math.log(0.02), math.log(1.0))), 0.02, 1.0)
    angles = jnp.clip(jax.random.uniform(streams_of[5], (2, DIRS), jnp.float32, -3.140625, 3.140625), -3.140625, 3.140625)
    wavenumbers = jnp.clip(jnp.exp(jax.random.uniform(streams_of[6], (NF,), jnp.float32, math.log(0.2), math.log(1.6))), 0.2, 1.6)
    return {"fields": fields, "material": material, "faces": faces, "permittivity": permittivity, "losses": losses, "angles": angles, "wavenumbers": wavenumbers}


COURANT = 0.5

def step_ahead(field, axis):
    count = field.shape[axis]
    later = lax.slice_in_dim(field, 1, count, axis=axis)
    edge = jnp.zeros_like(lax.slice_in_dim(field, 0, 1, axis=axis))
    return jnp.concatenate([later, edge], axis=axis) - field

def step_behind(field, axis):
    count = field.shape[axis]
    earlier = lax.slice_in_dim(field, 0, count - 1, axis=axis)
    edge = jnp.zeros_like(lax.slice_in_dim(field, 0, 1, axis=axis))
    return field - jnp.concatenate([edge, earlier], axis=axis)

def curl_of(vector, differ):
    first = vector[0]
    second = vector[1]
    third = vector[2]
    return jnp.stack([differ(third, 2) - differ(second, 0), differ(first, 0) - differ(third, 1), differ(second, 1) - differ(first, 2)])

def surface_rows(state, faces):
    masks = faces.astype(jnp.float32)
    normal_x = masks[0]
    normal_y = masks[1]
    normal_z = masks[2]
    channels = jnp.stack([-state[5] * normal_x, state[4] * normal_x, state[2] * normal_x, -state[1] * normal_x, state[5] * normal_y, -state[3] * normal_y, -state[2] * normal_y, state[0] * normal_y, -state[4] * normal_z, state[3] * normal_z, state[1] * normal_z, -state[0] * normal_z])
    depth, width, height = (channels.shape[1], channels.shape[2], channels.shape[3])
    shaped = channels.reshape(12, depth // 4, 4, width // 4, 4, height // 4, 4)
    return lax.optimization_barrier(jnp.mean(shaped, axis=(2, 4, 6))).astype(jnp.bfloat16)

def direction_table(angles, wavenumbers, tile_x, tile_y):
    polar_angle = angles[0]
    azimuth = angles[1]
    unit_x = jnp.sin(polar_angle) * jnp.cos(azimuth)
    unit_y = jnp.sin(polar_angle) * jnp.sin(azimuth)
    unit_z = jnp.cos(polar_angle)
    spots = jnp.arange(tile_x * tile_y, dtype=jnp.int32)
    offset_x = (spots // tile_y).astype(jnp.float32)
    offset_y = (spots % tile_y).astype(jnp.float32)
    phase = wavenumbers[:, None, None] * (unit_x[None, :, None] * offset_x[None, None, :] + unit_y[None, :, None] * offset_y[None, None, :])
    table = jnp.stack([jnp.cos(phase), jnp.sin(phase)]).astype(jnp.bfloat16)
    return (table, (unit_x, unit_y, unit_z))

def far_add(table, units, wavenumbers, pieces, start_x, start_y, start_z):
    grid = jnp.einsum('sfdk,jczk->sfdjcz', table, pieces, preferred_element_type=jnp.float32)
    layers = jnp.arange(pieces.shape[2], dtype=jnp.int32).astype(jnp.float32)
    unit_x, unit_y, unit_z = units
    lateral = unit_x[:, None] * start_x[None, :] + unit_y[:, None] * start_y[None, :]
    height = unit_z[:, None, None] * (start_z[None, :, None] + layers[None, None, :])
    phase = wavenumbers[:, None, None, None] * (lateral[None, :, :, None] + height[None])
    cosine = jnp.cos(phase)[:, :, :, None, :]
    sine = jnp.sin(phase)[:, :, :, None, :]
    real_sum = lax.optimization_barrier(jnp.sum(grid[0] * cosine - grid[1] * sine, axis=(2, 4)))
    imag_sum = lax.optimization_barrier(jnp.sum(grid[0] * sine + grid[1] * cosine, axis=(2, 4)))
    joined = jnp.stack([real_sum, imag_sum])
    return jnp.transpose(joined, (2, 0, 1, 3)).reshape(joined.shape[2], -1)

def reference(fields, material, faces, permittivity, losses, angles, wavenumbers):
    picked_loss = losses[material]
    picked_eps = permittivity[material]
    ratio_keep = (1.0 - picked_loss) / (1.0 + picked_loss)
    ratio_curl = COURANT / (picked_eps * (1.0 + picked_loss))
    state = fields
    for repeat in range(2):
        magnetic = state[3:] - COURANT * curl_of(state[:3], step_ahead)
        electric = ratio_keep * state[:3] + ratio_curl * curl_of(magnetic, step_behind)
        state = jnp.concatenate([electric, magnetic])
    rows = surface_rows(state, faces)
    tile_x = CX // 4
    tile_y = CY // 4
    layers = NZ // 4
    pieces = rows.reshape(12, layers, N_GX, tile_x, N_GY, tile_y)
    pieces = jnp.transpose(pieces, (2, 4, 0, 1, 3, 5)).reshape(N_GX * N_GY, 12, layers, tile_x * tile_y)
    pieces = pieces.astype(jnp.float32)
    order = jnp.arange(N_GX * N_GY, dtype=jnp.int32)
    start_x = (order // N_GY * tile_x).astype(jnp.float32)
    start_y = (order % N_GY * tile_y).astype(jnp.float32)
    start_z = jnp.zeros((N_GX * N_GY,), jnp.float32)
    block = 16 * DIR_DEV
    grouped = jnp.transpose(angles.reshape(2, DIRS // block, block), (1, 0, 2))

    def one_block(block_angles):
        table, units = direction_table(block_angles, wavenumbers, tile_x, tile_y)
        return far_add(table.astype(jnp.float32), units, wavenumbers, pieces, start_x, start_y, start_z)
    far = lax.map(one_block, grouped).reshape(DIRS, 24 * NF)
    scale = 8.0 / math.sqrt(NX // 4 * (NY // 4) * (NZ // 4))
    return (state, far * scale)
```

```python
import functools
import math

import jax
import jax.numpy as jnp
from jax import lax
from jax.experimental import pallas as pl
from jax.experimental.pallas import tpu as pltpu
from jax.sharding import PartitionSpec as P

MESH = pl.DeviceIdType.MESH
COURANT = 0.5
BLOCK = 4
CHANNELS = 12
ROWS = 16
AXES = ("gz", "gx", "gy")


def iota(shape, axis):
    return lax.broadcasted_iota(jnp.int32, shape, axis)


def split_dot(left, right):
    high = left.astype(jnp.bfloat16)
    low = (left - high.astype(jnp.float32)).astype(jnp.bfloat16)
    return jnp.dot(high, right, preferred_element_type=jnp.float32) + jnp.dot(
        low, right, preferred_element_type=jnp.float32
    )


def kernel(
    counts,
    dirs,
    fields_ref,
    material_ref,
    faces_ref,
    eps_ref,
    loss_ref,
    angles_ref,
    wave_ref,
    state_ref,
    far_ref,
    send_x,
    send_y,
    halo_z,
    halo_x,
    halo_y,
    gathered,
    send_sem,
    recv_sem,
    rows_send_sem,
    rows_recv_sem,
):
    n_gz, n_gx, n_gy = counts
    total = n_gz * n_gx * n_gy
    place = {axis: lax.axis_index(axis) for axis in AXES}
    at_z, at_x, at_y = (place[axis] for axis in AXES)
    me = (at_z * n_gx + at_x) * n_gy + at_y

    def coords(number):
        return {
            "gz": number // (n_gx * n_gy),
            "gx": (number // n_gy) % n_gx,
            "gy": number % n_gy,
        }

    barrier = pltpu.get_barrier_semaphore()

    def greet(step, carry):
        pl.semaphore_signal(
            barrier, inc=1, device_id=coords((me + step) % total), device_id_type=MESH
        )
        return carry

    lax.fori_loop(1, total, greet, 0)

    depth, width, height = fields_ref.shape[1:]
    plane = (width, height)
    lane = iota(plane, 1)
    row = iota(plane, 0)

    material = material_ref[...]
    loss = jnp.zeros(material.shape, jnp.float32)
    eps = jnp.zeros(material.shape, jnp.float32)
    for label in range(eps_ref.shape[0]):
        chosen = material == label
        loss = jnp.where(chosen, loss_ref[label], loss)
        eps = jnp.where(chosen, eps_ref[label], eps)
    keep = (1.0 - loss) / (1.0 + loss)
    gain = COURANT / (eps * (1.0 + loss))

    pl.semaphore_wait(barrier, total - 1)

    def exchange(stage, source, base, comps_x, comps_y, edge_z, edge_x, edge_y, by):
        for at, comp in enumerate(comps_x):
            for z in range(depth):
                k = at * depth + z
                send_x[stage, k : k + 1, :] = source[base + comp, z, edge_x : edge_x + 1, :]
        packed = jnp.zeros(plane, jnp.float32)
        for at, comp in enumerate(comps_y):
            for z in range(depth):
                column = source[base + comp, z, :, edge_y : edge_y + 1]
                packed = jnp.where(
                    lane == at * depth + z, jnp.broadcast_to(column, plane), packed
                )
        send_y[stage] = packed
        sources = (
            source.at[pl.ds(base, 2), edge_z],
            send_x.at[stage],
            send_y.at[stage],
        )
        targets = (halo_z.at[stage], halo_x.at[stage], halo_y.at[stage])
        copies = []
        for way, axis in enumerate(AXES):
            last = counts[way] - 1
            copies.append(
                pltpu.make_async_remote_copy(
                    src_ref=sources[way],
                    dst_ref=targets[way],
                    send_sem=send_sem.at[stage, way],
                    recv_sem=recv_sem.at[stage, way],
                    device_id={axis: place[axis] + by},
                    device_id_type=MESH,
                )
            )
            sends = place[axis] > 0 if by < 0 else place[axis] < last

            @pl.when(sends)
            def _():
                copies[way].start()

        return copies

    def land(copies, stage, by):
        halos = (halo_z, halo_x, halo_y)
        for way, axis in enumerate(AXES):
            last = counts[way] - 1
            sends = place[axis] > 0 if by < 0 else place[axis] < last
            takes = place[axis] < last if by < 0 else place[axis] > 0

            @pl.when(sends)
            def _():
                copies[way].wait_send()

            @pl.when(takes)
            def _():
                copies[way].wait_recv()

            @pl.when(jnp.logical_not(takes))
            def _():
                halos[way][stage] = jnp.zeros(halos[way].shape[1:], jnp.float32)

    def next_z(field, stage, at):
        return [field[z] for z in range(1, depth)] + [halo_z[stage, at]]

    def prev_z(field, stage, at):
        return [halo_z[stage, at]] + [field[z] for z in range(depth - 1)]

    def next_x(field, stage, at):
        out = []
        for z in range(depth):
            k = at * depth + z
            edge = jnp.broadcast_to(halo_x[stage, k : k + 1, :], plane)
            out.append(jnp.where(row == width - 1, edge, pltpu.roll(field[z], width - 1, 0)))
        return out

    def prev_x(field, stage, at):
        out = []
        for z in range(depth):
            k = at * depth + z
            edge = jnp.broadcast_to(halo_x[stage, k : k + 1, :], plane)
            out.append(jnp.where(row == 0, edge, pltpu.roll(field[z], 1, 0)))
        return out

    def next_y(field, stage, at):
        out = []
        for z in range(depth):
            k = at * depth + z
            edge = jnp.broadcast_to(halo_y[stage, :, k : k + 1], plane)
            out.append(jnp.where(lane == height - 1, edge, pltpu.roll(field[z], height - 1, 1)))
        return out

    def prev_y(field, stage, at):
        out = []
        for z in range(depth):
            k = at * depth + z
            edge = jnp.broadcast_to(halo_y[stage, :, k : k + 1], plane)
            out.append(jnp.where(lane == 0, edge, pltpu.roll(field[z], 1, 1)))
        return out

    def magnetic_step(source, stage):
        ex, ey, ez = ([source[c, z] for z in range(depth)] for c in range(3))
        ey_z, ex_z = next_z(ey, stage, 1), next_z(ex, stage, 0)
        ey_x, ez_x = next_x(ey, stage, 0), next_x(ez, stage, 1)
        ex_y, ez_y = next_y(ex, stage, 0), next_y(ez, stage, 1)
        for z in range(depth):
            curl = (
                (ez_y[z] - ez[z]) - (ey_z[z] - ey[z]),
                (ex_z[z] - ex[z]) - (ez_x[z] - ez[z]),
                (ey_x[z] - ey[z]) - (ex_y[z] - ex[z]),
            )
            for c in range(3):
                state_ref[3 + c, z] = source[3 + c, z] - COURANT * curl[c]

    def electric_step(source, stage):
        hx, hy, hz = ([state_ref[3 + c, z] for z in range(depth)] for c in range(3))
        hy_z, hx_z = prev_z(hy, stage, 1), prev_z(hx, stage, 0)
        hy_x, hz_x = prev_x(hy, stage, 0), prev_x(hz, stage, 1)
        hx_y, hz_y = prev_y(hx, stage, 0), prev_y(hz, stage, 1)
        for z in range(depth):
            curl = (
                (hz[z] - hz_y[z]) - (hy[z] - hy_z[z]),
                (hx[z] - hx_z[z]) - (hz[z] - hz_x[z]),
                (hy[z] - hy_x[z]) - (hx[z] - hx_y[z]),
            )
            for c in range(3):
                state_ref[c, z] = keep[z] * source[c, z] + gain[z] * curl[c]

    tile_x, tile_y = width // BLOCK, height // BLOCK
    spots = tile_x * tile_y
    freqs = wave_ref.shape[0]
    columns = 2 * freqs * dirs

    def steering():
        spot = iota((1, columns), 1)
        spot_d = spot % dirs
        spot_f = (spot // dirs) % freqs
        base = ((at_x * n_gy + at_y) * n_gz + at_z) * dirs
        polar = jnp.zeros((1, columns), jnp.float32)
        azimuth = jnp.zeros((1, columns), jnp.float32)
        wave = jnp.zeros((1, columns), jnp.float32)
        for d in range(dirs):
            polar = jnp.where(spot_d == d, angles_ref[0, base + d], polar)
            azimuth = jnp.where(spot_d == d, angles_ref[1, base + d], azimuth)
        for f in range(freqs):
            wave = jnp.where(spot_f == f, wave_ref[f], wave)
        unit_x = jnp.sin(polar) * jnp.cos(azimuth)
        unit_y = jnp.sin(polar) * jnp.sin(azimuth)
        unit_z = jnp.cos(polar)
        return wave, unit_x, unit_y, unit_z, spot

    def offset_table(steer):
        wave, unit_x, unit_y, unit_z, spot = steer
        cell = iota((spots, columns), 0)
        offset_x = (cell // tile_y).astype(jnp.float32)
        offset_y = (cell % tile_y).astype(jnp.float32)
        phase = wave * (unit_x * offset_x + unit_y * offset_y)
        quarter = jnp.where(spot >= columns // 2, math.pi / 2, 0.0)
        return jnp.cos(phase - quarter).astype(jnp.bfloat16)

    def tile_phases(steer):
        wave, unit_x, unit_y, unit_z, spot = steer
        tile = iota((total, columns), 0)
        start_z = (tile // (n_gx * n_gy)).astype(jnp.float32)
        start_x = ((tile // n_gy) % n_gx * tile_x).astype(jnp.float32)
        start_y = (tile % n_gy * tile_y).astype(jnp.float32)
        phase = wave * (unit_x * start_x + unit_y * start_y + unit_z * start_z)
        return jnp.cos(phase), jnp.sin(phase)

    copies = exchange(0, fields_ref, 0, (1, 2), (0, 2), 0, 0, 0, -1)
    steer = steering()
    land(copies, 0, -1)
    magnetic_step(fields_ref, 0)
    copies = exchange(1, state_ref, 3, (1, 2), (0, 2), depth - 1, width - 1, height - 1, 1)
    table = offset_table(steer)
    land(copies, 1, 1)
    electric_step(fields_ref, 1)
    copies = exchange(2, state_ref, 0, (1, 2), (0, 2), 0, 0, 0, -1)
    turn_cos, turn_sin = tile_phases(steer)
    land(copies, 2, -1)
    magnetic_step(state_ref, 2)
    copies = exchange(3, state_ref, 3, (1, 2), (0, 2), depth - 1, width - 1, height - 1, 1)
    masks = faces_ref[...].astype(jnp.float32)
    land(copies, 3, 1)
    electric_step(state_ref, 3)

    parts = (
        (5, 0, -1.0), (4, 0, 1.0), (2, 0, 1.0), (1, 0, -1.0),
        (5, 1, 1.0), (3, 1, -1.0), (2, 1, -1.0), (0, 1, 1.0),
        (4, 2, -1.0), (3, 2, 1.0), (1, 2, 1.0), (0, 2, -1.0),
    )
    sums = []
    for comp, normal, sign in parts:
        one = state_ref[comp, 0] * masks[normal, 0]
        for z in range(1, depth):
            one = one + state_ref[comp, z] * masks[normal, z]
        sums.append(one * (sign / BLOCK**3))
    stacked = jnp.concatenate(sums, axis=0)
    take = (iota((height, spots), 1) % tile_y == iota((height, spots), 0) // BLOCK)
    spread = split_dot(stacked, take.astype(jnp.float32).astype(jnp.bfloat16))
    own = iota((width, spots), 1) // tile_y == iota((width, spots), 0) // BLOCK
    own_rows = [
        jnp.sum(
            jnp.where(own, spread[c * width : (c + 1) * width], 0.0), axis=0, keepdims=True
        )
        for c in range(CHANNELS)
    ]
    own_rows.append(jnp.zeros((ROWS - CHANNELS, spots), jnp.float32))
    gathered[me] = jnp.concatenate(own_rows, axis=0).astype(jnp.bfloat16)

    def rows_copy(slot, other):
        return pltpu.make_async_remote_copy(
            src_ref=gathered.at[slot],
            dst_ref=gathered.at[slot],
            send_sem=rows_send_sem.at[other],
            recv_sem=rows_recv_sem.at[slot],
            device_id=coords(other),
            device_id_type=MESH,
        )

    def send_rows(step, carry):
        rows_copy(me, (me + step) % total).start()
        return carry

    def take_rows(step, carry):
        other = (me + step) % total
        rows_copy(other, other).wait_recv()
        rows_copy(me, other).wait_send()
        return carry

    lax.fori_loop(1, total, send_rows, 0)
    lax.fori_loop(1, total, take_rows, 0)

    grid = jnp.dot(
        gathered[...].reshape(total * ROWS, spots), table, preferred_element_type=jnp.float32
    ).reshape(total, ROWS, columns)
    by_cos = jnp.sum(grid * turn_cos[:, None, :], axis=0)
    by_sin = jnp.sum(grid * turn_sin[:, None, :], axis=0)
    half = columns // 2
    crossed = pltpu.roll(by_sin, half, 1)
    column = iota((ROWS, columns), 1)
    joined = jnp.where(column < half, by_cos - crossed, by_cos + crossed)
    scale = 8.0 / math.sqrt(total * spots)
    turned = jnp.transpose(joined * scale)
    for k in range(2 * freqs):
        far_ref[:, k * CHANNELS : (k + 1) * CHANNELS] = turned[k * dirs : (k + 1) * dirs, :CHANNELS]


def shards(counts, fields, material, faces, permittivity, losses, angles, wavenumbers):
    total = math.prod(counts)
    depth, width, height = fields.shape[1:]
    dirs = angles.shape[1] // total
    freqs = wavenumbers.shape[0]
    spots = (width // BLOCK) * (height // BLOCK)
    vmem = pl.BlockSpec(memory_space=pltpu.VMEM)
    smem = pl.BlockSpec(memory_space=pltpu.SMEM)
    return pl.pallas_call(
        functools.partial(kernel, counts, dirs),
        out_shape=(
            jax.ShapeDtypeStruct(fields.shape, jnp.float32),
            jax.ShapeDtypeStruct((dirs, 2 * freqs * CHANNELS), jnp.float32),
        ),
        in_specs=[vmem, vmem, vmem, smem, smem, smem, smem],
        out_specs=(vmem, vmem),
        scratch_shapes=[
            pltpu.VMEM((4, 2 * depth, height), jnp.float32),
            pltpu.VMEM((4, width, height), jnp.float32),
            pltpu.VMEM((4, 2, width, height), jnp.float32),
            pltpu.VMEM((4, 2 * depth, height), jnp.float32),
            pltpu.VMEM((4, width, height), jnp.float32),
            pltpu.VMEM((total, ROWS, spots), jnp.bfloat16),
            pltpu.SemaphoreType.DMA((4, 3)),
            pltpu.SemaphoreType.DMA((4, 3)),
            pltpu.SemaphoreType.DMA((total,)),
            pltpu.SemaphoreType.DMA((total,)),
        ],
        compiler_params=pltpu.CompilerParams(
            collective_id=0, has_side_effects=True, vmem_limit_bytes=48 * 1024 * 1024
        ),
    )(fields, material, faces, permittivity, losses, angles, wavenumbers)


def solution(mesh):
    counts = tuple(mesh.shape[axis] for axis in AXES)
    return jax.shard_map(
        functools.partial(shards, counts),
        mesh=mesh,
        in_specs=(
            P(None, "gz", "gx", "gy"),
            P("gz", "gx", "gy"),
            P(None, "gz", "gx", "gy"),
            P(),
            P(),
            P(),
            P(),
        ),
        out_specs=(P(None, "gz", "gx", "gy"), P(("gx", "gy", "gz"), None)),
        check_vma=False,
    )
```

```python
import functools
import math

import jax
import jax.numpy as jnp
from jax import lax
from jax.experimental import pallas as pl
from jax.experimental.pallas import tpu as pltpu
from jax.sharding import PartitionSpec as P

MESH = pl.DeviceIdType.MESH
COURANT = 0.5
BLOCK = 4
CHANNELS = 12
ROWS = 16
AXES = ("gz", "gx", "gy")


def iota(shape, axis):
    return lax.broadcasted_iota(jnp.int32, shape, axis)


def split_dot(left, right):
    high = left.astype(jnp.bfloat16)
    low = (left - high.astype(jnp.float32)).astype(jnp.bfloat16)
    return jnp.dot(high, right, preferred_element_type=jnp.float32) + jnp.dot(
        low, right, preferred_element_type=jnp.float32
    )


def kernel(
    counts,
    dirs,
    fields_hbm,
    material_hbm,
    faces_hbm,
    eps_hbm,
    loss_hbm,
    angles_hbm,
    wave_hbm,
    state_ref,
    far_ref,
    fields_ref,
    material_ref,
    faces_ref,
    eps_ref,
    loss_ref,
    angles_ref,
    wave_ref,
    send_x,
    send_y,
    halo_z,
    halo_x,
    halo_y,
    edge_zy,
    edge_zx,
    edge_xz,
    edge_xy,
    edge_yz,
    edge_yx,
    gathered,
    local_sem,
    send_sem,
    recv_sem,
    rows_send_sem,
    rows_recv_sem,
):
    n_gz, n_gx, n_gy = counts
    total = n_gz * n_gx * n_gy
    place = {axis: lax.axis_index(axis) for axis in AXES}
    at_z, at_x, at_y = (place[axis] for axis in AXES)
    me = (at_z * n_gx + at_x) * n_gy + at_y

    def coords(number):
        return {
            "gz": number // (n_gx * n_gy),
            "gx": (number // n_gy) % n_gx,
            "gy": number % n_gy,
        }

    pairs = (
        (fields_hbm, fields_ref),
        (material_hbm, material_ref),
        (loss_hbm, loss_ref),
        (eps_hbm, eps_ref),
        (angles_hbm, angles_ref),
        (wave_hbm, wave_ref),
        (faces_hbm, faces_ref),
    )
    loads = [pltpu.make_async_copy(a, b, local_sem.at[k]) for k, (a, b) in enumerate(pairs)]
    for load in loads:
        load.start()

    barrier = pltpu.get_barrier_semaphore()

    def greet(step, carry):
        pl.semaphore_signal(
            barrier, inc=1, device_id=coords((me + step) % total), device_id_type=MESH
        )
        return carry

    lax.fori_loop(1, total, greet, 0)

    depth, width, height = fields_ref.shape[1:]
    plane = (width, height)
    lane = iota(plane, 1)
    row = iota(plane, 0)
    levels = range(depth)

    def later_x(field):
        return [jnp.where(row == width - 1, 0.0, pltpu.roll(f, width - 1, 0)) for f in field]

    def later_y(field):
        return [jnp.where(lane == height - 1, 0.0, pltpu.roll(f, height - 1, 1)) for f in field]

    def magnetic_inside(source):
        ex, ey, ez = ([source[c, z] for z in levels] for c in range(3))
        none = jnp.zeros(plane, jnp.float32)
        ey_z, ex_z = ey[1:] + [none], ex[1:] + [none]
        ey_x, ez_x = later_x(ey), later_x(ez)
        ex_y, ez_y = later_y(ex), later_y(ez)
        for z in levels:
            curl = (
                (ez_y[z] - ez[z]) - (ey_z[z] - ey[z]),
                (ex_z[z] - ex[z]) - (ez_x[z] - ez[z]),
                (ey_x[z] - ey[z]) - (ex_y[z] - ex[z]),
            )
            for c in range(3):
                state_ref[3 + c, z] = source[3 + c, z] - COURANT * curl[c]

    def pack_faces(source, stage):
        for side, ref, base, edge_x, edge_y in (
            (0, source, 0, 0, 0),
            (1, state_ref, 3, width - 1, height - 1),
        ):
            for at, comp in enumerate((1, 2)):
                for z in levels:
                    k = at * depth + z
                    send_x[stage, side, k : k + 1, :] = ref[base + comp, z, edge_x : edge_x + 1, :]
            packed = jnp.zeros(plane, jnp.float32)
            for at, comp in enumerate((0, 2)):
                for z in levels:
                    column = ref[base + comp, z, :, edge_y : edge_y + 1]
                    packed = jnp.where(
                        lane == at * depth + z, jnp.broadcast_to(column, plane), packed
                    )
            send_y[stage, side] = packed

    def exchange(source, stage):
        low, high = pl.ds(0, 8), pl.ds(width - 8, 8)
        plan = (
            (source.at[pl.ds(0, 2), 0], halo_z.at[stage, 0], {"gz": -1}),
            (state_ref.at[pl.ds(3, 2), depth - 1], halo_z.at[stage, 1], {"gz": 1}),
            (source.at[2, depth - 1], edge_zy.at[stage], {"gz": 1, "gy": -1}),
            (source.at[2, depth - 1, low], edge_zx.at[stage], {"gz": 1, "gx": -1}),
            (source.at[0, 0, high], edge_xz.at[stage], {"gx": 1, "gz": -1}),
            (source.at[1, 0], edge_yz.at[stage], {"gy": 1, "gz": -1}),
            (send_x.at[stage, 0], halo_x.at[stage, 0], {"gx": -1}),
            (send_x.at[stage, 1], halo_x.at[stage, 1], {"gx": 1}),
            (send_y.at[stage, 0], halo_y.at[stage, 0], {"gy": -1}),
            (send_y.at[stage, 1], halo_y.at[stage, 1], {"gy": 1}),
            (source.at[0, :, high], edge_xy.at[stage], {"gx": 1, "gy": -1}),
            (source.at[1, :, low], edge_yx.at[stage], {"gy": 1, "gx": -1}),
        )
        out = []
        for number, (src, dst, move) in enumerate(plan):
            sends = takes = None
            for axis, by in move.items():
                last = counts[AXES.index(axis)] - 1
                up, down = place[axis] < last, place[axis] > 0
                send, take = (up, down) if by > 0 else (down, up)
                sends = send if sends is None else jnp.logical_and(sends, send)
                takes = take if takes is None else jnp.logical_and(takes, take)
            copy = pltpu.make_async_remote_copy(
                src_ref=src,
                dst_ref=dst,
                send_sem=send_sem.at[stage, number],
                recv_sem=recv_sem.at[stage, number],
                device_id={axis: place[axis] + by for axis, by in move.items()},
                device_id_type=MESH,
            )
            pl.when(sends)(copy.start)
            out.append((copy, dst, sends, takes))
        return out

    def land(copies):
        for copy, dst, sends, takes in copies:
            pl.when(takes)(copy.wait_recv)

            @pl.when(jnp.logical_not(takes))
            def _():
                dst[...] = jnp.zeros(dst.shape, jnp.float32)

        for copy, dst, sends, takes in copies:
            pl.when(sends)(copy.wait_send)

    def spread_row(line):
        return jnp.broadcast_to(line, plane)

    def complete(source, stage):
        half = COURANT
        last_row, last_lane = row == width - 1, lane == height - 1
        column = [[None] * depth for _ in range(4)]
        line = [[None] * depth for _ in range(4)]
        for k in range(2):
            for z in levels:
                n = k * depth + z
                for side in range(2):
                    column[2 * side + k][z] = jnp.broadcast_to(
                        halo_y[stage, side, :, n : n + 1], plane
                    )
                    line[2 * side + k][z] = halo_x[stage, side, n : n + 1, :]
        hx, hy, hz = ([state_ref[3 + c, z] for z in levels] for c in range(3))
        top = depth - 1
        for z in levels:
            ey_x, ez_x = spread_row(line[0][z]), spread_row(line[1][z])
            ex_y, ez_y = column[0][z], column[1][z]
            hx[z] = hx[z] - jnp.where(last_lane, half * ez_y, 0.0)
            hy[z] = hy[z] + jnp.where(last_row, half * ez_x, 0.0)
            hz[z] = hz[z] + (
                jnp.where(last_lane, half * ex_y, 0.0) - jnp.where(last_row, half * ey_x, 0.0)
            )
        hx[top] = hx[top] + half * halo_z[stage, 0, 1]
        hy[top] = hy[top] - half * halo_z[stage, 0, 0]
        for z in levels:
            state_ref[3, z] = hx[z]
            state_ref[4, z] = hy[z]
            state_ref[5, z] = hz[z]
        in_z = jnp.where(at_z > 0, half, 0.0)
        in_x = jnp.where(at_x > 0, half, 0.0)
        in_y = jnp.where(at_y > 0, half, 0.0)
        first = edge_zy[stage, :, 0:1]
        hx_z = (
            halo_z[stage, 1, 0]
            + in_z * source[1, 0]
            - jnp.where(last_lane, half * jnp.broadcast_to(first, plane), 0.0)
        )
        hy_z = (
            halo_z[stage, 1, 1]
            - in_z * source[0, 0]
            + jnp.where(last_row, half * spread_row(edge_zx[stage, 0:1, :]), 0.0)
        )
        lane_row = iota((1, height), 1)
        hy_x, hz_x = [], []
        for z in levels:
            low_y = line[2][z] + in_x * source[2, z, 0:1, :]
            if z == top:
                low_y = low_y - half * edge_xz[stage, 7:8, :]
            corner = jnp.broadcast_to(edge_xy[stage, z, 7:8, 0:1], (1, height))
            low_z = (
                line[3][z]
                - in_x * source[1, z, 0:1, :]
                + jnp.where(lane_row == height - 1, half * corner, 0.0)
            )
            hy_x.append(spread_row(low_y))
            hz_x.append(spread_row(low_z))
        hx_y, hz_y = [], []
        for z in levels:
            low_x = column[2][z] - in_y * jnp.broadcast_to(source[2, z, :, 0:1], plane)
            if z == top:
                final = edge_yz[stage, :, height - 1 : height]
                low_x = low_x + half * jnp.broadcast_to(final, plane)
            corner = jnp.broadcast_to(edge_yx[stage, z, 0:1, height - 1 : height], plane)
            low_z = (
                column[3][z]
                + in_y * jnp.broadcast_to(source[0, z, :, 0:1], plane)
                - jnp.where(last_row, half * corner, 0.0)
            )
            hx_y.append(low_x)
            hz_y.append(low_z)

        def before_x(field, edge):
            return [jnp.where(row == 0, e, pltpu.roll(f, 1, 0)) for f, e in zip(field, edge)]

        def before_y(field, edge):
            return [jnp.where(lane == 0, e, pltpu.roll(f, 1, 1)) for f, e in zip(field, edge)]

        hx_z, hy_z = [hx_z] + hx[:-1], [hy_z] + hy[:-1]
        hy_x, hz_x = before_x(hy, hy_x), before_x(hz, hz_x)
        hx_y, hz_y = before_y(hx, hx_y), before_y(hz, hz_y)
        for z in levels:
            curl = (
                (hz[z] - hz_y[z]) - (hy[z] - hy_z[z]),
                (hx[z] - hx_z[z]) - (hz[z] - hz_x[z]),
                (hy[z] - hy_x[z]) - (hx[z] - hx_y[z]),
            )
            for c in range(3):
                state_ref[c, z] = keep[z] * source[c, z] + gain[z] * curl[c]

    tile_x, tile_y = width // BLOCK, height // BLOCK
    spots = tile_x * tile_y
    freqs = wave_ref.shape[0]
    columns = 2 * freqs * dirs

    def steering():
        spot = iota((1, columns), 1)
        spot_d = spot % dirs
        spot_f = (spot // dirs) % freqs
        base = ((at_x * n_gy + at_y) * n_gz + at_z) * dirs
        polar = jnp.zeros((1, columns), jnp.float32)
        azimuth = jnp.zeros((1, columns), jnp.float32)
        wave = jnp.zeros((1, columns), jnp.float32)
        for d in range(dirs):
            polar = jnp.where(spot_d == d, angles_ref[0, base + d], polar)
            azimuth = jnp.where(spot_d == d, angles_ref[1, base + d], azimuth)
        for f in range(freqs):
            wave = jnp.where(spot_f == f, wave_ref[f], wave)
        unit_x = jnp.sin(polar) * jnp.cos(azimuth)
        unit_y = jnp.sin(polar) * jnp.sin(azimuth)
        unit_z = jnp.cos(polar)
        return wave, unit_x, unit_y, unit_z, spot

    def offset_table(steer):
        wave, unit_x, unit_y, unit_z, spot = steer
        cell = iota((spots, columns), 0)
        offset_x = (cell // tile_y).astype(jnp.float32)
        offset_y = (cell % tile_y).astype(jnp.float32)
        phase = wave * (unit_x * offset_x + unit_y * offset_y)
        quarter = jnp.where(spot >= columns // 2, math.pi / 2, 0.0)
        return jnp.cos(phase - quarter).astype(jnp.bfloat16)

    def tile_phases(steer):
        wave, unit_x, unit_y, unit_z, spot = steer
        tile = iota((total, columns), 0)
        start_z = (tile // (n_gx * n_gy)).astype(jnp.float32)
        start_x = ((tile // n_gy) % n_gx * tile_x).astype(jnp.float32)
        start_y = (tile % n_gy * tile_y).astype(jnp.float32)
        phase = wave * (unit_x * start_x + unit_y * start_y + unit_z * start_z)
        return jnp.cos(phase), jnp.sin(phase)

    loads[0].wait()
    magnetic_inside(fields_ref)
    pack_faces(fields_ref, 0)
    pl.semaphore_wait(barrier, total - 1)
    copies = exchange(fields_ref, 0)
    for load in loads[1:]:
        load.wait()
    material = material_ref[...]
    loss = jnp.zeros(material.shape, jnp.float32)
    eps = jnp.zeros(material.shape, jnp.float32)
    for label in range(eps_ref.shape[0]):
        chosen = material == label
        loss = jnp.where(chosen, loss_ref[label], loss)
        eps = jnp.where(chosen, eps_ref[label], eps)
    keep = (1.0 - loss) / (1.0 + loss)
    gain = COURANT / (eps * (1.0 + loss))
    steer = steering()
    turn_cos, turn_sin = tile_phases(steer)
    land(copies)
    complete(fields_ref, 0)
    old_ref = fields_ref
    for c in range(6):
        old_ref[c] = state_ref[c]
    magnetic_inside(old_ref)
    pack_faces(old_ref, 1)
    copies = exchange(old_ref, 1)
    masks = faces_ref[...].astype(jnp.float32)
    table = offset_table(steer)
    land(copies)
    complete(old_ref, 1)

    parts = (
        (5, 0, -1.0), (4, 0, 1.0), (2, 0, 1.0), (1, 0, -1.0),
        (5, 1, 1.0), (3, 1, -1.0), (2, 1, -1.0), (0, 1, 1.0),
        (4, 2, -1.0), (3, 2, 1.0), (1, 2, 1.0), (0, 2, -1.0),
    )
    sums = []
    for comp, normal, sign in parts:
        one = state_ref[comp, 0] * masks[normal, 0]
        for z in range(1, depth):
            one = one + state_ref[comp, z] * masks[normal, z]
        sums.append(one * (sign / BLOCK**3))
    stacked = jnp.concatenate(sums, axis=0)
    take = (iota((height, spots), 1) % tile_y == iota((height, spots), 0) // BLOCK)
    spread = split_dot(stacked, take.astype(jnp.float32).astype(jnp.bfloat16))
    own = iota((width, spots), 1) // tile_y == iota((width, spots), 0) // BLOCK
    own_rows = [
        jnp.sum(
            jnp.where(own, spread[c * width : (c + 1) * width], 0.0), axis=0, keepdims=True
        )
        for c in range(CHANNELS)
    ]
    own_rows.append(jnp.zeros((ROWS - CHANNELS, spots), jnp.float32))
    gathered[me] = jnp.concatenate(own_rows, axis=0).astype(jnp.bfloat16)

    def rows_copy(slot, other):
        return pltpu.make_async_remote_copy(
            src_ref=gathered.at[slot],
            dst_ref=gathered.at[slot],
            send_sem=rows_send_sem.at[other],
            recv_sem=rows_recv_sem.at[slot],
            device_id=coords(other),
            device_id_type=MESH,
        )

    def send_rows(step, carry):
        rows_copy(me, (me + step) % total).start()
        return carry

    def take_rows(step, carry):
        other = (me + step) % total
        rows_copy(other, other).wait_recv()
        rows_copy(me, other).wait_send()
        return carry

    lax.fori_loop(1, total, send_rows, 0)
    lax.fori_loop(1, total, take_rows, 0)

    grid = jnp.dot(
        gathered[...].reshape(total * ROWS, spots), table, preferred_element_type=jnp.float32
    ).reshape(total, ROWS, columns)
    by_cos = jnp.sum(grid * turn_cos[:, None, :], axis=0)
    by_sin = jnp.sum(grid * turn_sin[:, None, :], axis=0)
    half = columns // 2
    crossed = pltpu.roll(by_sin, half, 1)
    column = iota((ROWS, columns), 1)
    joined = jnp.where(column < half, by_cos - crossed, by_cos + crossed)
    scale = 8.0 / math.sqrt(total * spots)
    turned = jnp.transpose(joined * scale)
    for k in range(2 * freqs):
        far_ref[:, k * CHANNELS : (k + 1) * CHANNELS] = turned[k * dirs : (k + 1) * dirs, :CHANNELS]


def shards(counts, fields, material, faces, permittivity, losses, angles, wavenumbers):
    total = math.prod(counts)
    depth, width, height = fields.shape[1:]
    dirs = angles.shape[1] // total
    freqs = wavenumbers.shape[0]
    spots = (width // BLOCK) * (height // BLOCK)
    vmem = pl.BlockSpec(memory_space=pltpu.VMEM)
    return pl.pallas_call(
        functools.partial(kernel, counts, dirs),
        out_shape=(
            jax.ShapeDtypeStruct(fields.shape, jnp.float32),
            jax.ShapeDtypeStruct((dirs, 2 * freqs * CHANNELS), jnp.float32),
        ),
        in_specs=[pl.BlockSpec(memory_space=pl.ANY)] * 7,
        out_specs=(vmem, vmem),
        scratch_shapes=[
            pltpu.VMEM(fields.shape, jnp.float32),
            pltpu.VMEM(material.shape, jnp.int32),
            pltpu.VMEM(faces.shape, jnp.int32),
            pltpu.SMEM(permittivity.shape, jnp.float32),
            pltpu.SMEM(losses.shape, jnp.float32),
            pltpu.SMEM(angles.shape, jnp.float32),
            pltpu.SMEM(wavenumbers.shape, jnp.float32),
            pltpu.VMEM((2, 2, 2 * depth, height), jnp.float32),
            pltpu.VMEM((2, 2, width, height), jnp.float32),
            pltpu.VMEM((2, 2, 2, width, height), jnp.float32),
            pltpu.VMEM((2, 2, 2 * depth, height), jnp.float32),
            pltpu.VMEM((2, 2, width, height), jnp.float32),
            pltpu.VMEM((2, width, height), jnp.float32),
            pltpu.VMEM((2, 8, height), jnp.float32),
            pltpu.VMEM((2, 8, height), jnp.float32),
            pltpu.VMEM((2, depth, 8, height), jnp.float32),
            pltpu.VMEM((2, width, height), jnp.float32),
            pltpu.VMEM((2, depth, 8, height), jnp.float32),
            pltpu.VMEM((total, ROWS, spots), jnp.bfloat16),
            pltpu.SemaphoreType.DMA((7,)),
            pltpu.SemaphoreType.DMA((2, 12)),
            pltpu.SemaphoreType.DMA((2, 12)),
            pltpu.SemaphoreType.DMA((total,)),
            pltpu.SemaphoreType.DMA((total,)),
        ],
        compiler_params=pltpu.CompilerParams(
            collective_id=0, has_side_effects=True, vmem_limit_bytes=48 * 1024 * 1024
        ),
    )(fields, material, faces, permittivity, losses, angles, wavenumbers)


def solution(mesh):
    counts = tuple(mesh.shape[axis] for axis in AXES)
    return jax.shard_map(
        functools.partial(shards, counts),
        mesh=mesh,
        in_specs=(
            P(None, "gz", "gx", "gy"),
            P("gz", "gx", "gy"),
            P(None, "gz", "gx", "gy"),
            P(),
            P(),
            P(),
            P(),
        ),
        out_specs=(P(None, "gz", "gx", "gy"), P(("gx", "gy", "gz"), None)),
        check_vma=False,
    )
```

```python
import functools
import math

import jax
import jax.numpy as jnp
from jax import lax
from jax.experimental import pallas as pl
from jax.experimental.pallas import tpu as pltpu
from jax.sharding import PartitionSpec as P

MESH = pl.DeviceIdType.MESH
COURANT = 0.5
BLOCK = 4
CHANNELS = 12
ROWS = 16
AXES = ("gz", "gx", "gy")


def iota(shape, axis):
    return lax.broadcasted_iota(jnp.int32, shape, axis)


def split_dot(left, right):
    high = left.astype(jnp.bfloat16)
    low = (left - high.astype(jnp.float32)).astype(jnp.bfloat16)
    return jnp.dot(high, right, preferred_element_type=jnp.float32) + jnp.dot(
        low, right, preferred_element_type=jnp.float32
    )


def kernel(
    counts,
    dirs,
    fields_hbm,
    material_hbm,
    faces_hbm,
    eps_hbm,
    loss_hbm,
    angles_hbm,
    wave_hbm,
    state_hbm,
    far_ref,
    state_ref,
    fields_ref,
    material_ref,
    faces_ref,
    eps_ref,
    loss_ref,
    angles_ref,
    wave_ref,
    send_x,
    send_y,
    halo_z,
    halo_x,
    halo_y,
    edge_zy,
    edge_zx,
    edge_xz,
    edge_xy,
    edge_yz,
    edge_yx,
    gathered,
    local_sem,
    send_sem,
    recv_sem,
    rows_send_sem,
    rows_recv_sem,
):
    n_gz, n_gx, n_gy = counts
    total = n_gz * n_gx * n_gy
    place = {axis: lax.axis_index(axis) for axis in AXES}
    at_z, at_x, at_y = (place[axis] for axis in AXES)
    me = (at_z * n_gx + at_x) * n_gy + at_y

    def wrapped(at, by, count):
        moved = at + by
        return jnp.where(moved >= count, moved - count, moved)

    def each_partner(act):
        near = [
            (dx, wrapped(at_x, dx, n_gx), dy, wrapped(at_y, dy, n_gy))
            for dx in range(n_gx)
            for dy in range(n_gy)
        ]

        def level(dz):
            other_z = wrapped(at_z, dz, n_gz)
            for dx, other_x, dy, other_y in near:
                if isinstance(dz, int) and dz == dx == dy == 0:
                    continue
                number = (other_z * n_gx + other_x) * n_gy + other_y
                act({"gz": other_z, "gx": other_x, "gy": other_y}, number)

        if n_gz <= 4:
            for dz in sorted(range(1, n_gz), key=lambda dz: abs(2 * dz - n_gz)):
                level(dz)
        else:
            pl.loop(1, n_gz)(level)
        level(0)

    pairs = (
        (fields_hbm, fields_ref),
        (material_hbm, material_ref),
        (loss_hbm, loss_ref),
        (eps_hbm, eps_ref),
        (angles_hbm, angles_ref),
        (wave_hbm, wave_ref),
        (faces_hbm, faces_ref),
    )
    loads = [pltpu.make_async_copy(a, b, local_sem.at[k]) for k, (a, b) in enumerate(pairs)]
    for load in loads:
        load.start()

    barrier = pltpu.get_barrier_semaphore()

    def greet(other, number):
        pl.semaphore_signal(barrier, inc=1, device_id=other, device_id_type=MESH)

    each_partner(greet)

    depth, width, height = fields_ref.shape[1:]
    plane = (width, height)
    lane = iota(plane, 1)
    row = iota(plane, 0)
    levels = range(depth)

    def later_x(field):
        return [jnp.where(row == width - 1, 0.0, pltpu.roll(f, width - 1, 0)) for f in field]

    def later_y(field):
        return [jnp.where(lane == height - 1, 0.0, pltpu.roll(f, height - 1, 1)) for f in field]

    def magnetic_inside(source):
        ex, ey, ez = ([source[c, z] for z in levels] for c in range(3))
        none = jnp.zeros(plane, jnp.float32)
        ey_z, ex_z = ey[1:] + [none], ex[1:] + [none]
        ey_x, ez_x = later_x(ey), later_x(ez)
        ex_y, ez_y = later_y(ex), later_y(ez)
        for z in levels:
            curl = (
                (ez_y[z] - ez[z]) - (ey_z[z] - ey[z]),
                (ex_z[z] - ex[z]) - (ez_x[z] - ez[z]),
                (ey_x[z] - ey[z]) - (ex_y[z] - ex[z]),
            )
            for c in range(3):
                state_ref[3 + c, z] = source[3 + c, z] - COURANT * curl[c]

    def pack_faces(source, stage):
        for side, ref, base, edge_x, edge_y in (
            (0, source, 0, 0, 0),
            (1, state_ref, 3, width - 1, height - 1),
        ):
            for at, comp in enumerate((1, 2)):
                for z in levels:
                    k = at * depth + z
                    send_x[stage, side, k : k + 1, :] = ref[base + comp, z, edge_x : edge_x + 1, :]
            packed = jnp.zeros(plane, jnp.float32)
            for at, comp in enumerate((0, 2)):
                for z in levels:
                    column = ref[base + comp, z, :, edge_y : edge_y + 1]
                    packed = jnp.where(
                        lane == at * depth + z, jnp.broadcast_to(column, plane), packed
                    )
            send_y[stage, side] = packed

    def exchange(source, stage):
        low, high = pl.ds(0, 8), pl.ds(width - 8, 8)
        plan = (
            (source.at[pl.ds(0, 2), 0], halo_z.at[stage, 0], {"gz": -1}),
            (state_ref.at[pl.ds(3, 2), depth - 1], halo_z.at[stage, 1], {"gz": 1}),
            (source.at[2, depth - 1], edge_zy.at[stage], {"gz": 1, "gy": -1}),
            (source.at[2, depth - 1, low], edge_zx.at[stage], {"gz": 1, "gx": -1}),
            (source.at[0, 0, high], edge_xz.at[stage], {"gx": 1, "gz": -1}),
            (source.at[1, 0], edge_yz.at[stage], {"gy": 1, "gz": -1}),
            (send_x.at[stage, 0], halo_x.at[stage, 0], {"gx": -1}),
            (send_x.at[stage, 1], halo_x.at[stage, 1], {"gx": 1}),
            (send_y.at[stage, 0], halo_y.at[stage, 0], {"gy": -1}),
            (send_y.at[stage, 1], halo_y.at[stage, 1], {"gy": 1}),
            (source.at[0, :, high], edge_xy.at[stage], {"gx": 1, "gy": -1}),
            (source.at[1, :, low], edge_yx.at[stage], {"gy": 1, "gx": -1}),
        )
        out = []
        for number, (src, dst, move) in enumerate(plan):
            sends = takes = None
            for axis, by in move.items():
                last = counts[AXES.index(axis)] - 1
                up, down = place[axis] < last, place[axis] > 0
                send, take = (up, down) if by > 0 else (down, up)
                sends = send if sends is None else jnp.logical_and(sends, send)
                takes = take if takes is None else jnp.logical_and(takes, take)
            copy = pltpu.make_async_remote_copy(
                src_ref=src,
                dst_ref=dst,
                send_sem=send_sem.at[stage, number],
                recv_sem=recv_sem.at[stage, number],
                device_id={axis: place[axis] + by for axis, by in move.items()},
                device_id_type=MESH,
            )
            pl.when(sends)(copy.start)
            out.append((copy, dst, sends, takes))
        return out

    def land(copies):
        for copy, dst, sends, takes in copies:
            pl.when(takes)(copy.wait_recv)

            @pl.when(jnp.logical_not(takes))
            def _():
                dst[...] = jnp.zeros(dst.shape, jnp.float32)

        for copy, dst, sends, takes in copies:
            pl.when(sends)(copy.wait_send)

    def spread_row(line):
        return jnp.broadcast_to(line, plane)

    def complete(source, stage):
        half = COURANT
        last_row, last_lane = row == width - 1, lane == height - 1
        column = [[None] * depth for _ in range(4)]
        line = [[None] * depth for _ in range(4)]
        for k in range(2):
            for z in levels:
                n = k * depth + z
                for side in range(2):
                    column[2 * side + k][z] = jnp.broadcast_to(
                        halo_y[stage, side, :, n : n + 1], plane
                    )
                    line[2 * side + k][z] = halo_x[stage, side, n : n + 1, :]
        hx, hy, hz = ([state_ref[3 + c, z] for z in levels] for c in range(3))
        top = depth - 1
        for z in levels:
            ey_x, ez_x = spread_row(line[0][z]), spread_row(line[1][z])
            ex_y, ez_y = column[0][z], column[1][z]
            hx[z] = hx[z] - jnp.where(last_lane, half * ez_y, 0.0)
            hy[z] = hy[z] + jnp.where(last_row, half * ez_x, 0.0)
            hz[z] = hz[z] + (
                jnp.where(last_lane, half * ex_y, 0.0) - jnp.where(last_row, half * ey_x, 0.0)
            )
        hx[top] = hx[top] + half * halo_z[stage, 0, 1]
        hy[top] = hy[top] - half * halo_z[stage, 0, 0]
        for z in levels:
            state_ref[3, z] = hx[z]
            state_ref[4, z] = hy[z]
            state_ref[5, z] = hz[z]
        in_z = jnp.where(at_z > 0, half, 0.0)
        in_x = jnp.where(at_x > 0, half, 0.0)
        in_y = jnp.where(at_y > 0, half, 0.0)
        first = edge_zy[stage, :, 0:1]
        hx_z = (
            halo_z[stage, 1, 0]
            + in_z * source[1, 0]
            - jnp.where(last_lane, half * jnp.broadcast_to(first, plane), 0.0)
        )
        hy_z = (
            halo_z[stage, 1, 1]
            - in_z * source[0, 0]
            + jnp.where(last_row, half * spread_row(edge_zx[stage, 0:1, :]), 0.0)
        )
        lane_row = iota((1, height), 1)
        hy_x, hz_x = [], []
        for z in levels:
            low_y = line[2][z] + in_x * source[2, z, 0:1, :]
            if z == top:
                low_y = low_y - half * edge_xz[stage, 7:8, :]
            corner = jnp.broadcast_to(edge_xy[stage, z, 7:8, 0:1], (1, height))
            low_z = (
                line[3][z]
                - in_x * source[1, z, 0:1, :]
                + jnp.where(lane_row == height - 1, half * corner, 0.0)
            )
            hy_x.append(spread_row(low_y))
            hz_x.append(spread_row(low_z))
        hx_y, hz_y = [], []
        for z in levels:
            low_x = column[2][z] - in_y * jnp.broadcast_to(source[2, z, :, 0:1], plane)
            if z == top:
                final = edge_yz[stage, :, height - 1 : height]
                low_x = low_x + half * jnp.broadcast_to(final, plane)
            corner = jnp.broadcast_to(edge_yx[stage, z, 0:1, height - 1 : height], plane)
            low_z = (
                column[3][z]
                + in_y * jnp.broadcast_to(source[0, z, :, 0:1], plane)
                - jnp.where(last_row, half * corner, 0.0)
            )
            hx_y.append(low_x)
            hz_y.append(low_z)

        def before_x(field, edge):
            return [jnp.where(row == 0, e, pltpu.roll(f, 1, 0)) for f, e in zip(field, edge)]

        def before_y(field, edge):
            return [jnp.where(lane == 0, e, pltpu.roll(f, 1, 1)) for f, e in zip(field, edge)]

        hx_z, hy_z = [hx_z] + hx[:-1], [hy_z] + hy[:-1]
        hy_x, hz_x = before_x(hy, hy_x), before_x(hz, hz_x)
        hx_y, hz_y = before_y(hx, hx_y), before_y(hz, hz_y)
        for z in levels:
            curl = (
                (hz[z] - hz_y[z]) - (hy[z] - hy_z[z]),
                (hx[z] - hx_z[z]) - (hz[z] - hz_x[z]),
                (hy[z] - hy_x[z]) - (hx[z] - hx_y[z]),
            )
            for c in range(3):
                state_ref[c, z] = keep[z] * source[c, z] + gain[z] * curl[c]

    tile_x, tile_y = width // BLOCK, height // BLOCK
    spots = tile_x * tile_y
    freqs = wave_ref.shape[0]
    columns = 2 * freqs * dirs

    def steering():
        spot = iota((1, columns), 1)
        spot_d = spot % dirs
        spot_f = (spot // dirs) % freqs
        base = ((at_x * n_gy + at_y) * n_gz + at_z) * dirs
        polar = jnp.zeros((1, columns), jnp.float32)
        azimuth = jnp.zeros((1, columns), jnp.float32)
        wave = jnp.zeros((1, columns), jnp.float32)
        for d in range(dirs):
            polar = jnp.where(spot_d == d, angles_ref[0, base + d], polar)
            azimuth = jnp.where(spot_d == d, angles_ref[1, base + d], azimuth)
        for f in range(freqs):
            wave = jnp.where(spot_f == f, wave_ref[f], wave)
        unit_x = jnp.sin(polar) * jnp.cos(azimuth)
        unit_y = jnp.sin(polar) * jnp.sin(azimuth)
        unit_z = jnp.cos(polar)
        return wave, unit_x, unit_y, unit_z, spot

    def offset_table(steer):
        wave, unit_x, unit_y, unit_z, spot = steer
        cell = iota((spots, columns), 0)
        offset_x = (cell // tile_y).astype(jnp.float32)
        offset_y = (cell % tile_y).astype(jnp.float32)
        phase = wave * (unit_x * offset_x + unit_y * offset_y)
        quarter = jnp.where(spot >= columns // 2, math.pi / 2, 0.0)
        return jnp.cos(phase - quarter).astype(jnp.bfloat16)

    def tile_phases(steer):
        wave, unit_x, unit_y, unit_z, spot = steer
        tile = iota((total, columns), 0)
        start_z = (tile // (n_gx * n_gy)).astype(jnp.float32)
        start_x = ((tile // n_gy) % n_gx * tile_x).astype(jnp.float32)
        start_y = (tile % n_gy * tile_y).astype(jnp.float32)
        phase = wave * (unit_x * start_x + unit_y * start_y + unit_z * start_z)
        return jnp.cos(phase), jnp.sin(phase)

    loads[0].wait()
    magnetic_inside(fields_ref)
    pack_faces(fields_ref, 0)
    pl.semaphore_wait(barrier, total - 1)
    copies = exchange(fields_ref, 0)
    for load in loads[1:]:
        load.wait()
    material = material_ref[...]
    loss = jnp.zeros(material.shape, jnp.float32)
    eps = jnp.zeros(material.shape, jnp.float32)
    for label in range(eps_ref.shape[0]):
        chosen = material == label
        loss = jnp.where(chosen, loss_ref[label], loss)
        eps = jnp.where(chosen, eps_ref[label], eps)
    keep = (1.0 - loss) / (1.0 + loss)
    gain = COURANT / (eps * (1.0 + loss))
    steer = steering()
    turn_cos, turn_sin = tile_phases(steer)
    land(copies)
    complete(fields_ref, 0)
    old_ref = fields_ref
    for c in range(6):
        old_ref[c] = state_ref[c]
    magnetic_inside(old_ref)
    pack_faces(old_ref, 1)
    copies = exchange(old_ref, 1)
    masks = faces_ref[...].astype(jnp.float32)
    table = offset_table(steer)
    land(copies)
    complete(old_ref, 1)

    save = pltpu.make_async_copy(state_ref, state_hbm, local_sem.at[len(pairs)])
    save.start()

    parts = (
        (5, 0, -1.0), (4, 0, 1.0), (2, 0, 1.0), (1, 0, -1.0),
        (5, 1, 1.0), (3, 1, -1.0), (2, 1, -1.0), (0, 1, 1.0),
        (4, 2, -1.0), (3, 2, 1.0), (1, 2, 1.0), (0, 2, -1.0),
    )
    sums = []
    for comp, normal, sign in parts:
        one = state_ref[comp, 0] * masks[normal, 0]
        for z in range(1, depth):
            one = one + state_ref[comp, z] * masks[normal, z]
        sums.append(one * (sign / BLOCK**3))
    stacked = jnp.concatenate(sums, axis=0)
    take = (iota((height, spots), 1) % tile_y == iota((height, spots), 0) // BLOCK)
    spread = split_dot(stacked, take.astype(jnp.float32).astype(jnp.bfloat16))
    own = iota((width, spots), 1) // tile_y == iota((width, spots), 0) // BLOCK
    own_rows = [
        jnp.sum(
            jnp.where(own, spread[c * width : (c + 1) * width], 0.0), axis=0, keepdims=True
        )
        for c in range(CHANNELS)
    ]
    own_rows.append(jnp.zeros((ROWS - CHANNELS, spots), jnp.float32))
    gathered[me] = jnp.concatenate(own_rows, axis=0).astype(jnp.bfloat16)

    def rows_copy(slot, other, number):
        return pltpu.make_async_remote_copy(
            src_ref=gathered.at[slot],
            dst_ref=gathered.at[slot],
            send_sem=rows_send_sem.at[number],
            recv_sem=rows_recv_sem.at[slot],
            device_id=other,
            device_id_type=MESH,
        )

    def take_rows(other, number):
        rows_copy(number, other, number).wait_recv()

    def end_rows(other, number):
        rows_copy(me, other, number).wait_send()

    each_partner(lambda other, number: rows_copy(me, other, number).start())
    each_partner(take_rows)

    grid = jnp.dot(
        gathered[...].reshape(total * ROWS, spots), table, preferred_element_type=jnp.float32
    ).reshape(total, ROWS, columns)
    by_cos = jnp.sum(grid * turn_cos[:, None, :], axis=0)
    by_sin = jnp.sum(grid * turn_sin[:, None, :], axis=0)
    half = columns // 2
    crossed = pltpu.roll(by_sin, half, 1)
    column = iota((ROWS, columns), 1)
    joined = jnp.where(column < half, by_cos - crossed, by_cos + crossed)
    scale = 8.0 / math.sqrt(total * spots)
    turned = jnp.transpose(joined * scale)
    for k in range(2 * freqs):
        far_ref[:, k * CHANNELS : (k + 1) * CHANNELS] = turned[k * dirs : (k + 1) * dirs, :CHANNELS]
    each_partner(end_rows)
    save.wait()


def hand_over(*results):
    count = len(results)

    def body(*refs):
        sems = refs[2 * count]
        copies = [
            pltpu.make_async_copy(refs[k], refs[count + k], sems.at[k]) for k in range(count)
        ]
        for copy in copies:
            copy.start()
        for copy in copies:
            copy.wait()

    return pl.pallas_call(
        body,
        out_shape=tuple(jax.ShapeDtypeStruct(r.shape, r.dtype) for r in results),
        in_specs=[pl.BlockSpec(memory_space=pltpu.HBM)] * count,
        out_specs=(pl.BlockSpec(memory_space=pltpu.HBM),) * count,
        scratch_shapes=[pltpu.SemaphoreType.DMA((count,))],
        compiler_params=pltpu.CompilerParams(vmem_limit_bytes=60 * 1024 * 1024),
    )(*results)


def shards(counts, fields, material, faces, permittivity, losses, angles, wavenumbers):
    total = math.prod(counts)
    depth, width, height = fields.shape[1:]
    dirs = angles.shape[1] // total
    freqs = wavenumbers.shape[0]
    spots = (width // BLOCK) * (height // BLOCK)
    vmem = pl.BlockSpec(memory_space=pltpu.VMEM)
    results = pl.pallas_call(
        functools.partial(kernel, counts, dirs),
        out_shape=(
            jax.ShapeDtypeStruct(fields.shape, jnp.float32),
            jax.ShapeDtypeStruct((dirs, 2 * freqs * CHANNELS), jnp.float32),
        ),
        in_specs=[pl.BlockSpec(memory_space=pltpu.HBM)] * 7,
        out_specs=(pl.BlockSpec(memory_space=pltpu.HBM), vmem),
        scratch_shapes=[
            pltpu.VMEM(fields.shape, jnp.float32),
            pltpu.VMEM(fields.shape, jnp.float32),
            pltpu.VMEM(material.shape, jnp.int32),
            pltpu.VMEM(faces.shape, jnp.int32),
            pltpu.SMEM(permittivity.shape, jnp.float32),
            pltpu.SMEM(losses.shape, jnp.float32),
            pltpu.SMEM(angles.shape, jnp.float32),
            pltpu.SMEM(wavenumbers.shape, jnp.float32),
            pltpu.VMEM((2, 2, 2 * depth, height), jnp.float32),
            pltpu.VMEM((2, 2, width, height), jnp.float32),
            pltpu.VMEM((2, 2, 2, width, height), jnp.float32),
            pltpu.VMEM((2, 2, 2 * depth, height), jnp.float32),
            pltpu.VMEM((2, 2, width, height), jnp.float32),
            pltpu.VMEM((2, width, height), jnp.float32),
            pltpu.VMEM((2, 8, height), jnp.float32),
            pltpu.VMEM((2, 8, height), jnp.float32),
            pltpu.VMEM((2, depth, 8, height), jnp.float32),
            pltpu.VMEM((2, width, height), jnp.float32),
            pltpu.VMEM((2, depth, 8, height), jnp.float32),
            pltpu.VMEM((total, ROWS, spots), jnp.bfloat16),
            pltpu.SemaphoreType.DMA((8,)),
            pltpu.SemaphoreType.DMA((2, 12)),
            pltpu.SemaphoreType.DMA((2, 12)),
            pltpu.SemaphoreType.DMA((total,)),
            pltpu.SemaphoreType.DMA((total,)),
        ],
        compiler_params=pltpu.CompilerParams(
            collective_id=0, has_side_effects=True, vmem_limit_bytes=60 * 1024 * 1024
        ),
    )(fields, material, faces, permittivity, losses, angles, wavenumbers)
    return hand_over(*results)


def solution(mesh):
    counts = tuple(mesh.shape[axis] for axis in AXES)
    return jax.shard_map(
        functools.partial(shards, counts),
        mesh=mesh,
        in_specs=(
            P(None, "gz", "gx", "gy"),
            P("gz", "gx", "gy"),
            P(None, "gz", "gx", "gy"),
            P(),
            P(),
            P(),
            P(),
        ),
        out_specs=(P(None, "gz", "gx", "gy"), P(("gx", "gy", "gz"), None)),
        check_vma=False,
    )
```

```python
import functools
import math

import jax
import jax.numpy as jnp
from jax import lax
from jax.experimental import pallas as pl
from jax.experimental.pallas import tpu as pltpu
from jax.sharding import PartitionSpec as P

MESH = pl.DeviceIdType.MESH
COURANT = 0.5
BLOCK = 4
CHANNELS = 12
ROWS = 16
AXES = ("gz", "gx", "gy")


def iota(shape, axis):
    return lax.broadcasted_iota(jnp.int32, shape, axis)


def split_dot(left, right):
    high = left.astype(jnp.bfloat16)
    low = (left - high.astype(jnp.float32)).astype(jnp.bfloat16)
    return jnp.dot(high, right, preferred_element_type=jnp.float32) + jnp.dot(
        low, right, preferred_element_type=jnp.float32
    )


def sin_cos(angle):
    turns = jnp.floor(angle * (2 / math.pi) + 0.5)
    rest = angle - turns * 1.5703125
    rest = rest - turns * 4.837512969970703125e-4
    rest = rest - turns * 7.54978995489188216e-8
    square = rest * rest
    sine = -1.9515295891e-4 * square + 8.3321608736e-3
    sine = (sine * square - 1.6666654611e-1) * square * rest + rest
    cosine = 2.443315711809948e-5 * square - 1.388731625493765e-3
    cosine = (cosine * square + 4.166664568298827e-2) * square * square - 0.5 * square + 1.0
    quarter = turns.astype(jnp.int32)
    odd = (quarter & 1) == 1
    sin_out = jnp.where(odd, cosine, sine)
    cos_out = jnp.where(odd, sine, cosine)
    sin_out = jnp.where((quarter & 2) == 2, -sin_out, sin_out)
    cos_out = jnp.where(((quarter + 1) & 2) == 2, -cos_out, cos_out)
    return sin_out, cos_out


def kernel(
    counts,
    dirs,
    fields_hbm,
    material_hbm,
    faces_hbm,
    eps_hbm,
    loss_hbm,
    angles_hbm,
    wave_hbm,
    state_hbm,
    far_ref,
    state_ref,
    fields_ref,
    material_ref,
    faces_ref,
    eps_ref,
    loss_ref,
    angles_ref,
    wave_ref,
    send_x,
    send_y,
    halo_z,
    halo_x,
    halo_y,
    edge_zy,
    edge_zx,
    edge_xz,
    edge_xy,
    edge_yz,
    edge_yx,
    gathered,
    table_ref,
    part_out,
    part_in,
    local_sem,
    send_sem,
    recv_sem,
    rows_send_sem,
    rows_recv_sem,
    part_send_sem,
    part_recv_sem,
):
    n_gz, n_gx, n_gy = counts
    total = n_gz * n_gx * n_gy
    place = {axis: lax.axis_index(axis) for axis in AXES}
    at_z, at_x, at_y = (place[axis] for axis in AXES)
    me = at_x * n_gy + at_y
    in_plane = n_gx * n_gy

    def wrapped(at, by, count):
        moved = at + by
        return jnp.where(moved >= count, moved - count, moved)

    def each_in_plane(act):
        for dx in range(n_gx):
            for dy in range(n_gy):
                if dx or dy:
                    other_x, other_y = wrapped(at_x, dx, n_gx), wrapped(at_y, dy, n_gy)
                    act({"gx": other_x, "gy": other_y}, other_x * n_gy + other_y)

    levels_away = sorted(range(1, n_gz), key=lambda dz: abs(2 * dz - n_gz))

    pairs = (
        (fields_hbm, fields_ref),
        (material_hbm, material_ref),
        (loss_hbm, loss_ref),
        (eps_hbm, eps_ref),
        (angles_hbm, angles_ref),
        (wave_hbm, wave_ref),
        (faces_hbm, faces_ref),
    )
    loads = [pltpu.make_async_copy(a, b, local_sem.at[k]) for k, (a, b) in enumerate(pairs)]
    for load in loads:
        load.start()

    barrier = pltpu.get_barrier_semaphore()
    each_in_plane(
        lambda other, number: pl.semaphore_signal(
            barrier, inc=1, device_id=other, device_id_type=MESH
        )
    )
    for dz in levels_away:
        pl.semaphore_signal(
            barrier, inc=1, device_id={"gz": wrapped(at_z, dz, n_gz)}, device_id_type=MESH
        )
    greeted = n_gx * n_gy + n_gz - 2
    for axis, last in (("gx", n_gx - 1), ("gy", n_gy - 1)):
        for by in (-1, 1):
            there = jnp.logical_and(
                place["gz"] < n_gz - 1 if by > 0 else place["gz"] > 0,
                place[axis] > 0 if by > 0 else place[axis] < last,
            )
            other = {"gz": place["gz"] + by, axis: place[axis] - by}

            @pl.when(there)
            def _():
                pl.semaphore_signal(barrier, inc=1, device_id=other, device_id_type=MESH)

            greeted = greeted + jnp.where(there, 1, 0)

    depth, width, height = fields_ref.shape[1:]
    plane = (width, height)
    lane = iota(plane, 1)
    row = iota(plane, 0)
    levels = range(depth)

    def later_x(field):
        return [jnp.where(row == width - 1, 0.0, pltpu.roll(f, width - 1, 0)) for f in field]

    def later_y(field):
        return [jnp.where(lane == height - 1, 0.0, pltpu.roll(f, height - 1, 1)) for f in field]

    def magnetic_inside(source):
        ex, ey, ez = ([source[c, z] for z in levels] for c in range(3))
        none = jnp.zeros(plane, jnp.float32)
        ey_z, ex_z = ey[1:] + [none], ex[1:] + [none]
        ey_x, ez_x = later_x(ey), later_x(ez)
        ex_y, ez_y = later_y(ex), later_y(ez)
        for z in levels:
            curl = (
                (ez_y[z] - ez[z]) - (ey_z[z] - ey[z]),
                (ex_z[z] - ex[z]) - (ez_x[z] - ez[z]),
                (ey_x[z] - ey[z]) - (ex_y[z] - ex[z]),
            )
            for c in range(3):
                state_ref[3 + c, z] = source[3 + c, z] - COURANT * curl[c]

    def pack_faces(source, stage):
        for side, ref, base, edge_x, edge_y in (
            (0, source, 0, 0, 0),
            (1, state_ref, 3, width - 1, height - 1),
        ):
            for at, comp in enumerate((1, 2)):
                for z in levels:
                    k = at * depth + z
                    send_x[stage, side, k : k + 1, :] = ref[base + comp, z, edge_x : edge_x + 1, :]
            packed = jnp.zeros(plane, jnp.float32)
            for at, comp in enumerate((0, 2)):
                for z in levels:
                    column = ref[base + comp, z, :, edge_y : edge_y + 1]
                    packed = jnp.where(
                        lane == at * depth + z, jnp.broadcast_to(column, plane), packed
                    )
            send_y[stage, side] = packed

    def exchange(source, stage):
        low, high = pl.ds(0, 8), pl.ds(width - 8, 8)
        plan = (
            (source.at[pl.ds(0, 2), 0], halo_z.at[stage, 0], {"gz": -1}),
            (state_ref.at[pl.ds(3, 2), depth - 1], halo_z.at[stage, 1], {"gz": 1}),
            (source.at[2, depth - 1], edge_zy.at[stage], {"gz": 1, "gy": -1}),
            (source.at[2, depth - 1, low], edge_zx.at[stage], {"gz": 1, "gx": -1}),
            (source.at[0, 0, high], edge_xz.at[stage], {"gx": 1, "gz": -1}),
            (source.at[1, 0], edge_yz.at[stage], {"gy": 1, "gz": -1}),
            (send_x.at[stage, 0], halo_x.at[stage, 0], {"gx": -1}),
            (send_x.at[stage, 1], halo_x.at[stage, 1], {"gx": 1}),
            (send_y.at[stage, 0], halo_y.at[stage, 0], {"gy": -1}),
            (send_y.at[stage, 1], halo_y.at[stage, 1], {"gy": 1}),
            (source.at[0, :, high], edge_xy.at[stage], {"gx": 1, "gy": -1}),
            (source.at[1, :, low], edge_yx.at[stage], {"gy": 1, "gx": -1}),
        )
        out = []
        for number, (src, dst, move) in enumerate(plan):
            sends = takes = None
            for axis, by in move.items():
                last = counts[AXES.index(axis)] - 1
                up, down = place[axis] < last, place[axis] > 0
                send, take = (up, down) if by > 0 else (down, up)
                sends = send if sends is None else jnp.logical_and(sends, send)
                takes = take if takes is None else jnp.logical_and(takes, take)
            copy = pltpu.make_async_remote_copy(
                src_ref=src,
                dst_ref=dst,
                send_sem=send_sem.at[stage, number],
                recv_sem=recv_sem.at[stage, number],
                device_id={axis: place[axis] + by for axis, by in move.items()},
                device_id_type=MESH,
            )
            pl.when(sends)(copy.start)
            out.append((copy, dst, sends, takes))
        return out

    def land(copies):
        for copy, dst, sends, takes in copies:
            pl.when(takes)(copy.wait_recv)

            @pl.when(jnp.logical_not(takes))
            def _():
                dst[...] = jnp.zeros(dst.shape, jnp.float32)

        for copy, dst, sends, takes in copies:
            pl.when(sends)(copy.wait_send)

    def spread_row(line):
        return jnp.broadcast_to(line, plane)

    def complete(source, stage):
        half = COURANT
        last_row, last_lane = row == width - 1, lane == height - 1
        column = [[None] * depth for _ in range(4)]
        line = [[None] * depth for _ in range(4)]
        for k in range(2):
            for z in levels:
                n = k * depth + z
                for side in range(2):
                    column[2 * side + k][z] = jnp.broadcast_to(
                        halo_y[stage, side, :, n : n + 1], plane
                    )
                    line[2 * side + k][z] = halo_x[stage, side, n : n + 1, :]
        hx, hy, hz = ([state_ref[3 + c, z] for z in levels] for c in range(3))
        top = depth - 1
        for z in levels:
            ey_x, ez_x = spread_row(line[0][z]), spread_row(line[1][z])
            ex_y, ez_y = column[0][z], column[1][z]
            hx[z] = hx[z] - jnp.where(last_lane, half * ez_y, 0.0)
            hy[z] = hy[z] + jnp.where(last_row, half * ez_x, 0.0)
            hz[z] = hz[z] + (
                jnp.where(last_lane, half * ex_y, 0.0) - jnp.where(last_row, half * ey_x, 0.0)
            )
        hx[top] = hx[top] + half * halo_z[stage, 0, 1]
        hy[top] = hy[top] - half * halo_z[stage, 0, 0]
        for z in levels:
            state_ref[3, z] = hx[z]
            state_ref[4, z] = hy[z]
            state_ref[5, z] = hz[z]
        in_z = jnp.where(at_z > 0, half, 0.0)
        in_x = jnp.where(at_x > 0, half, 0.0)
        in_y = jnp.where(at_y > 0, half, 0.0)
        first = edge_zy[stage, :, 0:1]
        hx_z = (
            halo_z[stage, 1, 0]
            + in_z * source[1, 0]
            - jnp.where(last_lane, half * jnp.broadcast_to(first, plane), 0.0)
        )
        hy_z = (
            halo_z[stage, 1, 1]
            - in_z * source[0, 0]
            + jnp.where(last_row, half * spread_row(edge_zx[stage, 0:1, :]), 0.0)
        )
        lane_row = iota((1, height), 1)
        hy_x, hz_x = [], []
        for z in levels:
            low_y = line[2][z] + in_x * source[2, z, 0:1, :]
            if z == top:
                low_y = low_y - half * edge_xz[stage, 7:8, :]
            corner = jnp.broadcast_to(edge_xy[stage, z, 7:8, 0:1], (1, height))
            low_z = (
                line[3][z]
                - in_x * source[1, z, 0:1, :]
                + jnp.where(lane_row == height - 1, half * corner, 0.0)
            )
            hy_x.append(spread_row(low_y))
            hz_x.append(spread_row(low_z))
        hx_y, hz_y = [], []
        for z in levels:
            low_x = column[2][z] - in_y * jnp.broadcast_to(source[2, z, :, 0:1], plane)
            if z == top:
                final = edge_yz[stage, :, height - 1 : height]
                low_x = low_x + half * jnp.broadcast_to(final, plane)
            corner = jnp.broadcast_to(edge_yx[stage, z, 0:1, height - 1 : height], plane)
            low_z = (
                column[3][z]
                + in_y * jnp.broadcast_to(source[0, z, :, 0:1], plane)
                - jnp.where(last_row, half * corner, 0.0)
            )
            hx_y.append(low_x)
            hz_y.append(low_z)

        def before_x(field, edge):
            return [jnp.where(row == 0, e, pltpu.roll(f, 1, 0)) for f, e in zip(field, edge)]

        def before_y(field, edge):
            return [jnp.where(lane == 0, e, pltpu.roll(f, 1, 1)) for f, e in zip(field, edge)]

        hx_z, hy_z = [hx_z] + hx[:-1], [hy_z] + hy[:-1]
        hy_x, hz_x = before_x(hy, hy_x), before_x(hz, hz_x)
        hx_y, hz_y = before_y(hx, hx_y), before_y(hz, hz_y)
        for z in levels:
            curl = (
                (hz[z] - hz_y[z]) - (hy[z] - hy_z[z]),
                (hx[z] - hx_z[z]) - (hz[z] - hz_x[z]),
                (hy[z] - hy_x[z]) - (hx[z] - hx_y[z]),
            )
            for c in range(3):
                state_ref[c, z] = keep[z] * source[c, z] + gain[z] * curl[c]

    tile_x, tile_y = width // BLOCK, height // BLOCK
    spots = tile_x * tile_y
    freqs = wave_ref.shape[0]
    columns = 2 * freqs * dirs

    def steering(dz):
        spot = iota((1, columns), 1)
        spot_d = spot % dirs
        spot_f = (spot // dirs) % freqs
        base = (me * n_gz + wrapped(at_z, dz, n_gz)) * dirs
        polar = jnp.zeros((1, columns), jnp.float32)
        azimuth = jnp.zeros((1, columns), jnp.float32)
        wave = jnp.zeros((1, columns), jnp.float32)
        for d in range(dirs):
            polar = jnp.where(spot_d == d, angles_ref[0, base + d], polar)
            azimuth = jnp.where(spot_d == d, angles_ref[1, base + d], azimuth)
        for f in range(freqs):
            wave = jnp.where(spot_f == f, wave_ref[f], wave)
        sin_p, cos_p = sin_cos(polar)
        sin_a, cos_a = sin_cos(azimuth)
        unit_x, unit_y, unit_z = sin_p * cos_a, sin_p * sin_a, cos_p

        highs = tile_y // 8
        coarse = iota((tile_x * highs, columns), 0)
        low = iota((8, columns), 0).astype(jnp.float32)
        quarter = jnp.where(spot >= columns // 2, math.pi / 2, 0.0)
        sin_c, cos_c = sin_cos(
            wave
            * (
                unit_x * (coarse // highs).astype(jnp.float32)
                + unit_y * (coarse % highs * 8).astype(jnp.float32)
            )
            - quarter
        )
        sin_l, cos_l = sin_cos(wave * (unit_y * low))
        table = [
            cos_c[k : k + 1] * cos_l - sin_c[k : k + 1] * sin_l for k in range(tile_x * highs)
        ]
        table_ref[:, dz * columns : (dz + 1) * columns] = jnp.concatenate(table, axis=0).astype(
            jnp.bfloat16
        )
        tile = iota((in_plane, columns), 0)
        start_x = (tile // n_gy * tile_x).astype(jnp.float32)
        start_y = (tile % n_gy * tile_y).astype(jnp.float32)
        start_z = at_z.astype(jnp.float32)
        return sin_cos(wave * (unit_x * start_x + unit_y * start_y + unit_z * start_z))

    loads[0].wait()
    magnetic_inside(fields_ref)
    pack_faces(fields_ref, 0)
    pl.semaphore_wait(barrier, greeted)
    copies = exchange(fields_ref, 0)
    for load in loads[1:]:
        load.wait()
    material = material_ref[...]
    loss = jnp.zeros(material.shape, jnp.float32)
    eps = jnp.zeros(material.shape, jnp.float32)
    for label in range(eps_ref.shape[0]):
        chosen = material == label
        loss = jnp.where(chosen, loss_ref[label], loss)
        eps = jnp.where(chosen, eps_ref[label], eps)
    keep = (1.0 - loss) / (1.0 + loss)
    gain = COURANT / (eps * (1.0 + loss))
    turns = {dz: steering(dz) for dz in levels_away[: len(levels_away) // 2 + 1]}
    land(copies)
    complete(fields_ref, 0)
    old_ref = fields_ref
    for c in range(6):
        old_ref[c] = state_ref[c]
    magnetic_inside(old_ref)
    pack_faces(old_ref, 1)
    copies = exchange(old_ref, 1)
    masks = faces_ref[...].astype(jnp.float32)
    for dz in range(n_gz):
        if dz not in turns:
            turns[dz] = steering(dz)
    land(copies)
    complete(old_ref, 1)

    save = pltpu.make_async_copy(state_ref, state_hbm, local_sem.at[len(pairs)])
    save.start()

    parts = (
        (5, 0, -1.0), (4, 0, 1.0), (2, 0, 1.0), (1, 0, -1.0),
        (5, 1, 1.0), (3, 1, -1.0), (2, 1, -1.0), (0, 1, 1.0),
        (4, 2, -1.0), (3, 2, 1.0), (1, 2, 1.0), (0, 2, -1.0),
    )
    sums = []
    for comp, normal, sign in parts:
        one = state_ref[comp, 0] * masks[normal, 0]
        for z in range(1, depth):
            one = one + state_ref[comp, z] * masks[normal, z]
        sums.append(one * (sign / BLOCK**3))
    stacked = jnp.concatenate(sums, axis=0)
    take = (iota((height, spots), 1) % tile_y == iota((height, spots), 0) // BLOCK)
    spread = split_dot(stacked, take.astype(jnp.float32).astype(jnp.bfloat16))
    own = iota((width, spots), 1) // tile_y == iota((width, spots), 0) // BLOCK
    own_rows = [
        jnp.sum(
            jnp.where(own, spread[c * width : (c + 1) * width], 0.0), axis=0, keepdims=True
        )
        for c in range(CHANNELS)
    ]
    own_rows.append(jnp.zeros((ROWS - CHANNELS, spots), jnp.float32))
    gathered[me] = jnp.concatenate(own_rows, axis=0).astype(jnp.bfloat16)

    def rows_copy(slot, other, number):
        return pltpu.make_async_remote_copy(
            src_ref=gathered.at[slot],
            dst_ref=gathered.at[slot],
            send_sem=rows_send_sem.at[number],
            recv_sem=rows_recv_sem.at[slot],
            device_id=other,
            device_id_type=MESH,
        )

    each_in_plane(lambda other, number: rows_copy(me, other, number).start())
    each_in_plane(lambda other, number: rows_copy(number, other, number).wait_recv())

    grid = jnp.dot(
        gathered[...].reshape(in_plane * ROWS, spots),
        table_ref[...],
        preferred_element_type=jnp.float32,
    )
    half = columns // 2
    column = iota((ROWS, columns), 1)
    scale = 8.0 / math.sqrt(total * spots)

    def part(dz):
        turn_sin, turn_cos = turns[dz]
        own = grid[:, dz * columns : (dz + 1) * columns]
        by_cos = by_sin = None
        for tile in range(in_plane):
            block = own[tile * ROWS : (tile + 1) * ROWS]
            one, two = block * turn_cos[tile : tile + 1], block * turn_sin[tile : tile + 1]
            by_cos = one if by_cos is None else by_cos + one
            by_sin = two if by_sin is None else by_sin + two
        crossed = pltpu.roll(by_sin, half, 1)
        return jnp.where(column < half, by_cos - crossed, by_cos + crossed) * scale

    def part_copy(dz):
        return pltpu.make_async_remote_copy(
            src_ref=part_out.at[dz - 1],
            dst_ref=part_in.at[dz - 1],
            send_sem=part_send_sem.at[dz - 1],
            recv_sem=part_recv_sem.at[dz - 1],
            device_id={"gz": wrapped(at_z, dz, n_gz)},
            device_id_type=MESH,
        )

    for dz in levels_away:
        part_out[dz - 1] = part(dz)
        part_copy(dz).start()
    far = part(0)
    for dz in levels_away:
        part_copy(dz).wait_recv()
        far = far + part_in[dz - 1]
    turned = jnp.transpose(far)
    for k in range(2 * freqs):
        far_ref[:, k * CHANNELS : (k + 1) * CHANNELS] = turned[k * dirs : (k + 1) * dirs, :CHANNELS]
    for dz in levels_away:
        part_copy(dz).wait_send()
    each_in_plane(lambda other, number: rows_copy(me, other, number).wait_send())
    save.wait()


def hand_over(*results):
    count = len(results)

    def body(*refs):
        for k in range(count):
            refs[count + k][...] = refs[k][...]

    vmem = pl.BlockSpec(memory_space=pltpu.VMEM)
    return pl.pallas_call(
        body,
        out_shape=tuple(jax.ShapeDtypeStruct(r.shape, r.dtype) for r in results),
        in_specs=[vmem] * count,
        out_specs=(vmem,) * count,
        compiler_params=pltpu.CompilerParams(vmem_limit_bytes=60 * 1024 * 1024),
    )(*results)


def shards(counts, fields, material, faces, permittivity, losses, angles, wavenumbers):
    total = math.prod(counts)
    depth, width, height = fields.shape[1:]
    dirs = angles.shape[1] // total
    freqs = wavenumbers.shape[0]
    n_gz, n_gx, n_gy = counts
    columns = 2 * freqs * dirs
    spots = (width // BLOCK) * (height // BLOCK)
    vmem = pl.BlockSpec(memory_space=pltpu.VMEM)
    results = pl.pallas_call(
        functools.partial(kernel, counts, dirs),
        out_shape=(
            jax.ShapeDtypeStruct(fields.shape, jnp.float32),
            jax.ShapeDtypeStruct((dirs, 2 * freqs * CHANNELS), jnp.float32),
        ),
        in_specs=[pl.BlockSpec(memory_space=pltpu.HBM)] * 7,
        out_specs=(pl.BlockSpec(memory_space=pltpu.HBM), vmem),
        scratch_shapes=[
            pltpu.VMEM(fields.shape, jnp.float32),
            pltpu.VMEM(fields.shape, jnp.float32),
            pltpu.VMEM(material.shape, jnp.int32),
            pltpu.VMEM(faces.shape, jnp.int32),
            pltpu.SMEM(permittivity.shape, jnp.float32),
            pltpu.SMEM(losses.shape, jnp.float32),
            pltpu.SMEM(angles.shape, jnp.float32),
            pltpu.SMEM(wavenumbers.shape, jnp.float32),
            pltpu.VMEM((2, 2, 2 * depth, height), jnp.float32),
            pltpu.VMEM((2, 2, width, height), jnp.float32),
            pltpu.VMEM((2, 2, 2, width, height), jnp.float32),
            pltpu.VMEM((2, 2, 2 * depth, height), jnp.float32),
            pltpu.VMEM((2, 2, width, height), jnp.float32),
            pltpu.VMEM((2, width, height), jnp.float32),
            pltpu.VMEM((2, 8, height), jnp.float32),
            pltpu.VMEM((2, 8, height), jnp.float32),
            pltpu.VMEM((2, depth, 8, height), jnp.float32),
            pltpu.VMEM((2, width, height), jnp.float32),
            pltpu.VMEM((2, depth, 8, height), jnp.float32),
            pltpu.VMEM((n_gx * n_gy, ROWS, spots), jnp.bfloat16),
            pltpu.VMEM((spots, n_gz * columns), jnp.bfloat16),
            pltpu.VMEM((max(n_gz - 1, 1), ROWS, columns), jnp.float32),
            pltpu.VMEM((max(n_gz - 1, 1), ROWS, columns), jnp.float32),
            pltpu.SemaphoreType.DMA((8,)),
            pltpu.SemaphoreType.DMA((2, 12)),
            pltpu.SemaphoreType.DMA((2, 12)),
            pltpu.SemaphoreType.DMA((n_gx * n_gy,)),
            pltpu.SemaphoreType.DMA((n_gx * n_gy,)),
            pltpu.SemaphoreType.DMA((max(n_gz - 1, 1),)),
            pltpu.SemaphoreType.DMA((max(n_gz - 1, 1),)),
        ],
        compiler_params=pltpu.CompilerParams(
            collective_id=0, has_side_effects=True, vmem_limit_bytes=60 * 1024 * 1024
        ),
    )(fields, material, faces, permittivity, losses, angles, wavenumbers)
    return hand_over(*results)


def solution(mesh):
    counts = tuple(mesh.shape[axis] for axis in AXES)
    return jax.shard_map(
        functools.partial(shards, counts),
        mesh=mesh,
        in_specs=(
            P(None, "gz", "gx", "gy"),
            P("gz", "gx", "gy"),
            P(None, "gz", "gx", "gy"),
            P(),
            P(),
            P(),
            P(),
        ),
        out_specs=(P(None, "gz", "gx", "gy"), P(("gx", "gy", "gz"), None)),
        check_vma=False,
    )
```

```python
import functools
import math

import jax
import jax.numpy as jnp
from jax import lax
from jax.experimental import pallas as pl
from jax.experimental.pallas import tpu as pltpu
from jax.sharding import PartitionSpec as P

MESH = pl.DeviceIdType.MESH
COURANT = 0.5
BLOCK = 4
CHANNELS = 12
ROWS = 16
AXES = ("gz", "gx", "gy")


def iota(shape, axis):
    return lax.broadcasted_iota(jnp.int32, shape, axis)


def split_dot(left, right):
    high = left.astype(jnp.bfloat16)
    low = (left - high.astype(jnp.float32)).astype(jnp.bfloat16)
    return jnp.dot(high, right, preferred_element_type=jnp.float32) + jnp.dot(
        low, right, preferred_element_type=jnp.float32
    )


def sin_cos(angle):
    turns = jnp.floor(angle * (2 / math.pi) + 0.5)
    rest = angle - turns * 1.5703125
    rest = rest - turns * 4.837512969970703125e-4
    rest = rest - turns * 7.54978995489188216e-8
    square = rest * rest
    sine = -1.9515295891e-4 * square + 8.3321608736e-3
    sine = (sine * square - 1.6666654611e-1) * square * rest + rest
    cosine = 2.443315711809948e-5 * square - 1.388731625493765e-3
    cosine = (cosine * square + 4.166664568298827e-2) * square * square - 0.5 * square + 1.0
    quarter = turns.astype(jnp.int32)
    odd = (quarter & 1) == 1
    sin_out = jnp.where(odd, cosine, sine)
    cos_out = jnp.where(odd, sine, cosine)
    sin_out = jnp.where((quarter & 2) == 2, -sin_out, sin_out)
    cos_out = jnp.where(((quarter + 1) & 2) == 2, -cos_out, cos_out)
    return sin_out, cos_out


def kernel(
    counts,
    dirs,
    fields_hbm,
    material_hbm,
    faces_hbm,
    eps_hbm,
    loss_hbm,
    angles_hbm,
    wave_hbm,
    state_ref,
    far_ref,
    mid_ref,
    inner_ref,
    fields_ref,
    material_ref,
    faces_ref,
    eps_ref,
    loss_ref,
    angles_ref,
    wave_ref,
    send_x,
    send_y,
    halo_z,
    halo_x,
    halo_y,
    edge_zy,
    edge_zx,
    edge_xz,
    edge_xy,
    edge_yz,
    edge_yx,
    gathered,
    table_ref,
    part_out,
    part_in,
    local_sem,
    send_sem,
    recv_sem,
    rows_send_sem,
    rows_recv_sem,
    part_send_sem,
    part_recv_sem,
):
    n_gz, n_gx, n_gy = counts
    total = n_gz * n_gx * n_gy
    place = {axis: lax.axis_index(axis) for axis in AXES}
    at_z, at_x, at_y = (place[axis] for axis in AXES)
    me = at_x * n_gy + at_y
    in_plane = n_gx * n_gy

    def wrapped(at, by, count):
        moved = at + by
        return jnp.where(moved >= count, moved - count, moved)

    def each_in_plane(act):
        for dx in range(n_gx):
            for dy in range(n_gy):
                if dx or dy:
                    other_x, other_y = wrapped(at_x, dx, n_gx), wrapped(at_y, dy, n_gy)
                    act({"gx": other_x, "gy": other_y}, other_x * n_gy + other_y)

    levels_away = sorted(range(1, n_gz), key=lambda dz: abs(2 * dz - n_gz))

    pairs = (
        (fields_hbm, fields_ref),
        (material_hbm, material_ref),
        (loss_hbm, loss_ref),
        (eps_hbm, eps_ref),
        (angles_hbm, angles_ref),
        (wave_hbm, wave_ref),
        (faces_hbm, faces_ref),
    )
    loads = [pltpu.make_async_copy(a, b, local_sem.at[k]) for k, (a, b) in enumerate(pairs)]
    for load in loads:
        load.start()

    halos = (halo_z, halo_x, halo_y, edge_zy, edge_zx, edge_xz, edge_xy, edge_yz, edge_yx)
    for halo in halos:
        halo[...] = jnp.zeros(halo.shape, jnp.float32)

    barrier = pltpu.get_barrier_semaphore()
    each_in_plane(
        lambda other, number: pl.semaphore_signal(
            barrier, inc=1, device_id=other, device_id_type=MESH
        )
    )
    for dz in levels_away:
        pl.semaphore_signal(
            barrier, inc=1, device_id={"gz": wrapped(at_z, dz, n_gz)}, device_id_type=MESH
        )
    greeted = n_gx * n_gy + n_gz - 2
    for axis, last in (("gx", n_gx - 1), ("gy", n_gy - 1)):
        for by in (-1, 1):
            there = jnp.logical_and(
                place["gz"] < n_gz - 1 if by > 0 else place["gz"] > 0,
                place[axis] > 0 if by > 0 else place[axis] < last,
            )
            other = {"gz": place["gz"] + by, axis: place[axis] - by}

            @pl.when(there)
            def _():
                pl.semaphore_signal(barrier, inc=1, device_id=other, device_id_type=MESH)

            greeted = greeted + jnp.where(there, 1, 0)

    depth, width, height = fields_ref.shape[1:]
    plane = (width, height)
    lane = iota(plane, 1)
    row = iota(plane, 0)
    levels = range(depth)

    def later_x(field):
        return [jnp.where(row == width - 1, 0.0, pltpu.roll(f, width - 1, 0)) for f in field]

    def later_y(field):
        return [jnp.where(lane == height - 1, 0.0, pltpu.roll(f, height - 1, 1)) for f in field]

    def magnetic_inside(source, stage):
        ex, ey, ez = ([source[c, z] for z in levels] for c in range(3))
        none = jnp.zeros(plane, jnp.float32)
        ey_z, ex_z = ey[1:] + [none], ex[1:] + [none]
        ey_x, ez_x = later_x(ey), later_x(ez)
        ex_y, ez_y = later_y(ex), later_y(ez)
        for z in levels:
            curl = (
                (ez_y[z] - ez[z]) - (ey_z[z] - ey[z]),
                (ex_z[z] - ex[z]) - (ez_x[z] - ez[z]),
                (ey_x[z] - ey[z]) - (ex_y[z] - ex[z]),
            )
            for c in range(3):
                inner_ref[stage, c, z] = source[3 + c, z] - COURANT * curl[c]

    def pack_faces(source, stage):
        for side, ref, edge_x, edge_y in (
            (0, source, 0, 0),
            (1, inner_ref.at[stage], width - 1, height - 1),
        ):
            for at, comp in enumerate((1, 2)):
                for z in levels:
                    k = at * depth + z
                    send_x[stage, side, k : k + 1, :] = ref[comp, z, edge_x : edge_x + 1, :]
            packed = jnp.zeros(plane, jnp.float32)
            for at, comp in enumerate((0, 2)):
                for z in levels:
                    column = ref[comp, z, :, edge_y : edge_y + 1]
                    packed = jnp.where(
                        lane == at * depth + z, jnp.broadcast_to(column, plane), packed
                    )
            send_y[stage, side] = packed

    def exchange(source, stage):
        low, high = pl.ds(0, 8), pl.ds(width - 8, 8)
        plan = (
            (source.at[pl.ds(0, 2), 0], halo_z.at[stage, 0], {"gz": -1}),
            (inner_ref.at[stage, pl.ds(0, 2), depth - 1], halo_z.at[stage, 1], {"gz": 1}),
            (source.at[2, depth - 1], edge_zy.at[stage], {"gz": 1, "gy": -1}),
            (source.at[2, depth - 1, low], edge_zx.at[stage], {"gz": 1, "gx": -1}),
            (source.at[0, 0, high], edge_xz.at[stage], {"gx": 1, "gz": -1}),
            (source.at[1, 0], edge_yz.at[stage], {"gy": 1, "gz": -1}),
            (send_x.at[stage, 0], halo_x.at[stage, 0], {"gx": -1}),
            (send_x.at[stage, 1], halo_x.at[stage, 1], {"gx": 1}),
            (send_y.at[stage, 0], halo_y.at[stage, 0], {"gy": -1}),
            (send_y.at[stage, 1], halo_y.at[stage, 1], {"gy": 1}),
            (source.at[0, :, high], edge_xy.at[stage], {"gx": 1, "gy": -1}),
            (source.at[1, :, low], edge_yx.at[stage], {"gy": 1, "gx": -1}),
        )
        out = []
        for number, (src, dst, move) in enumerate(plan):
            sends = takes = None
            for axis, by in move.items():
                last = counts[AXES.index(axis)] - 1
                up, down = place[axis] < last, place[axis] > 0
                send, take = (up, down) if by > 0 else (down, up)
                sends = send if sends is None else jnp.logical_and(sends, send)
                takes = take if takes is None else jnp.logical_and(takes, take)
            copy = pltpu.make_async_remote_copy(
                src_ref=src,
                dst_ref=dst,
                send_sem=send_sem.at[stage, number],
                recv_sem=recv_sem.at[stage, number],
                device_id={axis: place[axis] + by for axis, by in move.items()},
                device_id_type=MESH,
            )
            pl.when(sends)(copy.start)
            out.append((copy, dst, sends, takes))
        return out

    def land(copies):
        for copy, dst, sends, takes in copies:
            pl.when(takes)(copy.wait_recv)

    def spread_row(line):
        return jnp.broadcast_to(line, plane)

    def complete(source, target, stage):
        half = COURANT
        last_row, last_lane = row == width - 1, lane == height - 1
        column = [[None] * depth for _ in range(4)]
        line = [[None] * depth for _ in range(4)]
        for k in range(2):
            for z in levels:
                n = k * depth + z
                for side in range(2):
                    column[2 * side + k][z] = jnp.broadcast_to(
                        halo_y[stage, side, :, n : n + 1], plane
                    )
                    line[2 * side + k][z] = halo_x[stage, side, n : n + 1, :]
        hx, hy, hz = ([inner_ref[stage, c, z] for z in levels] for c in range(3))
        top = depth - 1
        for z in levels:
            ey_x, ez_x = spread_row(line[0][z]), spread_row(line[1][z])
            ex_y, ez_y = column[0][z], column[1][z]
            hx[z] = hx[z] - jnp.where(last_lane, half * ez_y, 0.0)
            hy[z] = hy[z] + jnp.where(last_row, half * ez_x, 0.0)
            hz[z] = hz[z] + (
                jnp.where(last_lane, half * ex_y, 0.0) - jnp.where(last_row, half * ey_x, 0.0)
            )
        hx[top] = hx[top] + half * halo_z[stage, 0, 1]
        hy[top] = hy[top] - half * halo_z[stage, 0, 0]
        for z in levels:
            target[3, z] = hx[z]
            target[4, z] = hy[z]
            target[5, z] = hz[z]
        in_z = jnp.where(at_z > 0, half, 0.0)
        in_x = jnp.where(at_x > 0, half, 0.0)
        in_y = jnp.where(at_y > 0, half, 0.0)
        first = edge_zy[stage, :, 0:1]
        hx_z = (
            halo_z[stage, 1, 0]
            + in_z * source[1, 0]
            - jnp.where(last_lane, half * jnp.broadcast_to(first, plane), 0.0)
        )
        hy_z = (
            halo_z[stage, 1, 1]
            - in_z * source[0, 0]
            + jnp.where(last_row, half * spread_row(edge_zx[stage, 0:1, :]), 0.0)
        )
        lane_row = iota((1, height), 1)
        hy_x, hz_x = [], []
        for z in levels:
            low_y = line[2][z] + in_x * source[2, z, 0:1, :]
            if z == top:
                low_y = low_y - half * edge_xz[stage, 7:8, :]
            corner = jnp.broadcast_to(edge_xy[stage, z, 7:8, 0:1], (1, height))
            low_z = (
                line[3][z]
                - in_x * source[1, z, 0:1, :]
                + jnp.where(lane_row == height - 1, half * corner, 0.0)
            )
            hy_x.append(spread_row(low_y))
            hz_x.append(spread_row(low_z))
        hx_y, hz_y = [], []
        for z in levels:
            low_x = column[2][z] - in_y * jnp.broadcast_to(source[2, z, :, 0:1], plane)
            if z == top:
                final = edge_yz[stage, :, height - 1 : height]
                low_x = low_x + half * jnp.broadcast_to(final, plane)
            corner = jnp.broadcast_to(edge_yx[stage, z, 0:1, height - 1 : height], plane)
            low_z = (
                column[3][z]
                + in_y * jnp.broadcast_to(source[0, z, :, 0:1], plane)
                - jnp.where(last_row, half * corner, 0.0)
            )
            hx_y.append(low_x)
            hz_y.append(low_z)

        def before_x(field, edge):
            return [jnp.where(row == 0, e, pltpu.roll(f, 1, 0)) for f, e in zip(field, edge)]

        def before_y(field, edge):
            return [jnp.where(lane == 0, e, pltpu.roll(f, 1, 1)) for f, e in zip(field, edge)]

        hx_z, hy_z = [hx_z] + hx[:-1], [hy_z] + hy[:-1]
        hy_x, hz_x = before_x(hy, hy_x), before_x(hz, hz_x)
        hx_y, hz_y = before_y(hx, hx_y), before_y(hz, hz_y)
        for z in levels:
            curl = (
                (hz[z] - hz_y[z]) - (hy[z] - hy_z[z]),
                (hx[z] - hx_z[z]) - (hz[z] - hz_x[z]),
                (hy[z] - hy_x[z]) - (hx[z] - hx_y[z]),
            )
            for c in range(3):
                target[c, z] = keep[z] * source[c, z] + gain[z] * curl[c]

    tile_x, tile_y = width // BLOCK, height // BLOCK
    spots = tile_x * tile_y
    freqs = wave_ref.shape[0]
    columns = 2 * freqs * dirs

    def steering(dz):
        spot = iota((1, columns), 1)
        spot_d = spot % dirs
        spot_f = (spot // dirs) % freqs
        base = (me * n_gz + wrapped(at_z, dz, n_gz)) * dirs
        polar = jnp.zeros((1, columns), jnp.float32)
        azimuth = jnp.zeros((1, columns), jnp.float32)
        wave = jnp.zeros((1, columns), jnp.float32)
        for d in range(dirs):
            polar = jnp.where(spot_d == d, angles_ref[0, base + d], polar)
            azimuth = jnp.where(spot_d == d, angles_ref[1, base + d], azimuth)
        for f in range(freqs):
            wave = jnp.where(spot_f == f, wave_ref[f], wave)
        sin_p, cos_p = sin_cos(polar)
        sin_a, cos_a = sin_cos(azimuth)
        unit_x, unit_y, unit_z = sin_p * cos_a, sin_p * sin_a, cos_p

        highs = tile_y // 8
        coarse = iota((tile_x * highs, columns), 0)
        low = iota((8, columns), 0).astype(jnp.float32)
        quarter = jnp.where(spot >= columns // 2, math.pi / 2, 0.0)
        sin_c, cos_c = sin_cos(
            wave
            * (
                unit_x * (coarse // highs).astype(jnp.float32)
                + unit_y * (coarse % highs * 8).astype(jnp.float32)
            )
            - quarter
        )
        sin_l, cos_l = sin_cos(wave * (unit_y * low))
        table = [
            cos_c[k : k + 1] * cos_l - sin_c[k : k + 1] * sin_l for k in range(tile_x * highs)
        ]
        table_ref[:, dz * columns : (dz + 1) * columns] = jnp.concatenate(table, axis=0).astype(
            jnp.bfloat16
        )
        tile = iota((in_plane, columns), 0)
        start_x = (tile // n_gy * tile_x).astype(jnp.float32)
        start_y = (tile % n_gy * tile_y).astype(jnp.float32)
        start_z = at_z.astype(jnp.float32)
        return sin_cos(wave * (unit_x * start_x + unit_y * start_y + unit_z * start_z))

    loads[0].wait()
    magnetic_inside(fields_ref, 0)
    pack_faces(fields_ref, 0)
    pl.semaphore_wait(barrier, greeted)
    first = exchange(fields_ref, 0)
    for load in loads[1:]:
        load.wait()
    material = material_ref[...]
    loss = jnp.zeros(material.shape, jnp.float32)
    eps = jnp.zeros(material.shape, jnp.float32)
    for label in range(eps_ref.shape[0]):
        chosen = material == label
        loss = jnp.where(chosen, loss_ref[label], loss)
        eps = jnp.where(chosen, eps_ref[label], eps)
    keep = (1.0 - loss) / (1.0 + loss)
    gain = COURANT / (eps * (1.0 + loss))
    turns = {dz: steering(dz) for dz in levels_away[: len(levels_away) // 2 + 1]}
    land(first)
    complete(fields_ref, mid_ref, 0)
    magnetic_inside(mid_ref, 1)
    pack_faces(mid_ref, 1)
    second = exchange(mid_ref, 1)
    masks = faces_ref[...].astype(jnp.float32)
    for dz in range(n_gz):
        if dz not in turns:
            turns[dz] = steering(dz)
    land(second)
    complete(mid_ref, state_ref, 1)

    parts = (
        (5, 0, -1.0), (4, 0, 1.0), (2, 0, 1.0), (1, 0, -1.0),
        (5, 1, 1.0), (3, 1, -1.0), (2, 1, -1.0), (0, 1, 1.0),
        (4, 2, -1.0), (3, 2, 1.0), (1, 2, 1.0), (0, 2, -1.0),
    )
    sums = []
    for comp, normal, sign in parts:
        one = state_ref[comp, 0] * masks[normal, 0]
        for z in range(1, depth):
            one = one + state_ref[comp, z] * masks[normal, z]
        sums.append(one * (sign / BLOCK**3))
    stacked = jnp.concatenate(sums, axis=0)
    take = (iota((height, spots), 1) % tile_y == iota((height, spots), 0) // BLOCK)
    spread = split_dot(stacked, take.astype(jnp.float32).astype(jnp.bfloat16))
    own = iota((width, spots), 1) // tile_y == iota((width, spots), 0) // BLOCK
    own_rows = [
        jnp.sum(
            jnp.where(own, spread[c * width : (c + 1) * width], 0.0), axis=0, keepdims=True
        )
        for c in range(CHANNELS)
    ]
    own_rows.append(jnp.zeros((ROWS - CHANNELS, spots), jnp.float32))
    gathered[me] = jnp.concatenate(own_rows, axis=0).astype(jnp.bfloat16)

    def rows_copy(slot, other, number):
        return pltpu.make_async_remote_copy(
            src_ref=gathered.at[slot],
            dst_ref=gathered.at[slot],
            send_sem=rows_send_sem.at[number],
            recv_sem=rows_recv_sem.at[slot],
            device_id=other,
            device_id_type=MESH,
        )

    each_in_plane(lambda other, number: rows_copy(me, other, number).start())
    each_in_plane(lambda other, number: rows_copy(number, other, number).wait_recv())

    grid = jnp.dot(
        gathered[...].reshape(in_plane * ROWS, spots),
        table_ref[...],
        preferred_element_type=jnp.float32,
    )
    half = columns // 2
    column = iota((ROWS, columns), 1)
    scale = 8.0 / math.sqrt(total * spots)

    def part(dz):
        turn_sin, turn_cos = turns[dz]
        own = grid[:, dz * columns : (dz + 1) * columns]
        by_cos = by_sin = None
        for tile in range(in_plane):
            block = own[tile * ROWS : (tile + 1) * ROWS]
            one, two = block * turn_cos[tile : tile + 1], block * turn_sin[tile : tile + 1]
            by_cos = one if by_cos is None else by_cos + one
            by_sin = two if by_sin is None else by_sin + two
        crossed = pltpu.roll(by_sin, half, 1)
        return jnp.where(column < half, by_cos - crossed, by_cos + crossed) * scale

    def part_copy(dz):
        return pltpu.make_async_remote_copy(
            src_ref=part_out.at[dz - 1],
            dst_ref=part_in.at[dz - 1],
            send_sem=part_send_sem.at[dz - 1],
            recv_sem=part_recv_sem.at[dz - 1],
            device_id={"gz": wrapped(at_z, dz, n_gz)},
            device_id_type=MESH,
        )

    for dz in levels_away:
        part_out[dz - 1] = part(dz)
        part_copy(dz).start()
    far = part(0)
    for copy, dst, sends, takes in first + second:
        pl.when(sends)(copy.wait_send)
    each_in_plane(lambda other, number: rows_copy(me, other, number).wait_send())
    for dz in levels_away:
        part_copy(dz).wait_recv()
        far = far + part_in[dz - 1]
    turned = jnp.transpose(far)
    for k in range(2 * freqs):
        far_ref[:, k * CHANNELS : (k + 1) * CHANNELS] = turned[k * dirs : (k + 1) * dirs, :CHANNELS]
    for dz in levels_away:
        part_copy(dz).wait_send()


def hand_over(*results):
    count = len(results)

    def body(*refs):
        sems = refs[2 * count]
        copies = [
            pltpu.make_async_copy(refs[k], refs[count + k], sems.at[k]) for k in range(count)
        ]
        for copy in copies:
            copy.start()
        for copy in copies:
            copy.wait()

    return pl.pallas_call(
        body,
        out_shape=tuple(jax.ShapeDtypeStruct(r.shape, r.dtype) for r in results),
        in_specs=[pl.BlockSpec(memory_space=pl.ANY)] * count,
        out_specs=(pl.BlockSpec(memory_space=pltpu.HBM),) * count,
        scratch_shapes=[pltpu.SemaphoreType.DMA((count,))],
        compiler_params=pltpu.CompilerParams(vmem_limit_bytes=1024 * 1024),
    )(*results)


def shards(counts, fields, material, faces, permittivity, losses, angles, wavenumbers):
    total = math.prod(counts)
    depth, width, height = fields.shape[1:]
    dirs = angles.shape[1] // total
    freqs = wavenumbers.shape[0]
    n_gz, n_gx, n_gy = counts
    columns = 2 * freqs * dirs
    spots = (width // BLOCK) * (height // BLOCK)
    vmem = pl.BlockSpec(memory_space=pltpu.VMEM)
    results = pl.pallas_call(
        functools.partial(kernel, counts, dirs),
        out_shape=(
            pltpu.VMEM(fields.shape, jnp.float32),
            pltpu.VMEM((dirs, 2 * freqs * CHANNELS), jnp.float32),
        ),
        in_specs=[pl.BlockSpec(memory_space=pltpu.HBM)] * 7,
        out_specs=(vmem, vmem),
        scratch_shapes=[
            pltpu.VMEM(fields.shape, jnp.float32),
            pltpu.VMEM((2, 3) + fields.shape[1:], jnp.float32),
            pltpu.VMEM(fields.shape, jnp.float32),
            pltpu.VMEM(material.shape, jnp.int32),
            pltpu.VMEM(faces.shape, jnp.int32),
            pltpu.SMEM(permittivity.shape, jnp.float32),
            pltpu.SMEM(losses.shape, jnp.float32),
            pltpu.SMEM(angles.shape, jnp.float32),
            pltpu.SMEM(wavenumbers.shape, jnp.float32),
            pltpu.VMEM((2, 2, 2 * depth, height), jnp.float32),
            pltpu.VMEM((2, 2, width, height), jnp.float32),
            pltpu.VMEM((2, 2, 2, width, height), jnp.float32),
            pltpu.VMEM((2, 2, 2 * depth, height), jnp.float32),
            pltpu.VMEM((2, 2, width, height), jnp.float32),
            pltpu.VMEM((2, width, height), jnp.float32),
            pltpu.VMEM((2, 8, height), jnp.float32),
            pltpu.VMEM((2, 8, height), jnp.float32),
            pltpu.VMEM((2, depth, 8, height), jnp.float32),
            pltpu.VMEM((2, width, height), jnp.float32),
            pltpu.VMEM((2, depth, 8, height), jnp.float32),
            pltpu.VMEM((n_gx * n_gy, ROWS, spots), jnp.bfloat16),
            pltpu.VMEM((spots, n_gz * columns), jnp.bfloat16),
            pltpu.VMEM((max(n_gz - 1, 1), ROWS, columns), jnp.float32),
            pltpu.VMEM((max(n_gz - 1, 1), ROWS, columns), jnp.float32),
            pltpu.SemaphoreType.DMA((7,)),
            pltpu.SemaphoreType.DMA((2, 12)),
            pltpu.SemaphoreType.DMA((2, 12)),
            pltpu.SemaphoreType.DMA((n_gx * n_gy,)),
            pltpu.SemaphoreType.DMA((n_gx * n_gy,)),
            pltpu.SemaphoreType.DMA((max(n_gz - 1, 1),)),
            pltpu.SemaphoreType.DMA((max(n_gz - 1, 1),)),
        ],
        compiler_params=pltpu.CompilerParams(
            collective_id=0, has_side_effects=True, vmem_limit_bytes=60 * 1024 * 1024
        ),
    )(fields, material, faces, permittivity, losses, angles, wavenumbers)
    return hand_over(*results)


def solution(mesh):
    counts = tuple(mesh.shape[axis] for axis in AXES)
    return jax.shard_map(
        functools.partial(shards, counts),
        mesh=mesh,
        in_specs=(
            P(None, "gz", "gx", "gy"),
            P("gz", "gx", "gy"),
            P(None, "gz", "gx", "gy"),
            P(),
            P(),
            P(),
            P(),
        ),
        out_specs=(P(None, "gz", "gx", "gy"), P(("gx", "gy", "gz"), None)),
        check_vma=False,
    )
```

```python
import functools
import math

import jax
import jax.numpy as jnp
from jax import lax
from jax.experimental import pallas as pl
from jax.experimental.pallas import tpu as pltpu
from jax.sharding import PartitionSpec as P

MESH = pl.DeviceIdType.MESH
COURANT = 0.5
BLOCK = 4
CHANNELS = 12
ROWS = 16
AXES = ("gz", "gx", "gy")


def iota(shape, axis):
    return lax.broadcasted_iota(jnp.int32, shape, axis)


def split_dot(left, right):
    high = left.astype(jnp.bfloat16)
    low = (left - high.astype(jnp.float32)).astype(jnp.bfloat16)
    return jnp.dot(high, right, preferred_element_type=jnp.float32) + jnp.dot(
        low, right, preferred_element_type=jnp.float32
    )


def sin_cos(angle):
    turns = jnp.floor(angle * (2 / math.pi) + 0.5)
    rest = angle - turns * 1.5703125
    rest = rest - turns * 4.837512969970703125e-4
    rest = rest - turns * 7.54978995489188216e-8
    square = rest * rest
    sine = -1.9515295891e-4 * square + 8.3321608736e-3
    sine = (sine * square - 1.6666654611e-1) * square * rest + rest
    cosine = 2.443315711809948e-5 * square - 1.388731625493765e-3
    cosine = (cosine * square + 4.166664568298827e-2) * square * square - 0.5 * square + 1.0
    quarter = turns.astype(jnp.int32)
    odd = (quarter & 1) == 1
    sin_out = jnp.where(odd, cosine, sine)
    cos_out = jnp.where(odd, sine, cosine)
    sin_out = jnp.where((quarter & 2) == 2, -sin_out, sin_out)
    cos_out = jnp.where(((quarter + 1) & 2) == 2, -cos_out, cos_out)
    return sin_out, cos_out


def kernel(
    counts,
    dirs,
    fields_hbm,
    material_hbm,
    faces_hbm,
    eps_hbm,
    loss_hbm,
    angles_hbm,
    wave_hbm,
    state_ref,
    far_ref,
    mid_ref,
    inner_ref,
    fields_ref,
    material_ref,
    faces_ref,
    eps_ref,
    loss_ref,
    angles_ref,
    wave_ref,
    send_x,
    send_y,
    halo_z,
    halo_x,
    halo_y,
    edge_zy,
    edge_zx,
    edge_xz,
    edge_xy,
    edge_yz,
    edge_yx,
    gathered,
    table_ref,
    part_out,
    part_in,
    local_sem,
    send_sem,
    recv_sem,
    rows_send_sem,
    rows_recv_sem,
    part_send_sem,
    part_recv_sem,
):
    n_gz, n_gx, n_gy = counts
    total = n_gz * n_gx * n_gy
    place = {axis: lax.axis_index(axis) for axis in AXES}
    at_z, at_x, at_y = (place[axis] for axis in AXES)
    me = at_x * n_gy + at_y
    in_plane = n_gx * n_gy

    def wrapped(at, by, count):
        moved = at + by
        return jnp.where(moved >= count, moved - count, moved)

    def each_in_plane(act):
        for dx in range(n_gx):
            for dy in range(n_gy):
                if dx or dy:
                    other_x, other_y = wrapped(at_x, dx, n_gx), wrapped(at_y, dy, n_gy)
                    act({"gx": other_x, "gy": other_y}, other_x * n_gy + other_y)

    levels_away = sorted(range(1, n_gz), key=lambda dz: abs(2 * dz - n_gz))

    pairs = (
        (fields_hbm, fields_ref),
        (material_hbm, material_ref),
        (loss_hbm, loss_ref),
        (eps_hbm, eps_ref),
        (angles_hbm, angles_ref),
        (wave_hbm, wave_ref),
        (faces_hbm, faces_ref),
    )
    loads = [pltpu.make_async_copy(a, b, local_sem.at[k]) for k, (a, b) in enumerate(pairs)]
    loads[0].start()

    halos = (halo_z, halo_x, halo_y, edge_zy, edge_zx, edge_xz, edge_xy, edge_yz, edge_yx)
    for halo in halos:
        halo[...] = jnp.zeros(halo.shape, jnp.float32)

    barrier = pltpu.get_barrier_semaphore()
    each_in_plane(
        lambda other, number: pl.semaphore_signal(
            barrier, inc=1, device_id=other, device_id_type=MESH
        )
    )
    for dz in levels_away:
        pl.semaphore_signal(
            barrier, inc=1, device_id={"gz": wrapped(at_z, dz, n_gz)}, device_id_type=MESH
        )
    greeted = n_gx * n_gy + n_gz - 2
    for axis, last in (("gx", n_gx - 1), ("gy", n_gy - 1)):
        for by in (-1, 1):
            there = jnp.logical_and(
                place["gz"] < n_gz - 1 if by > 0 else place["gz"] > 0,
                place[axis] > 0 if by > 0 else place[axis] < last,
            )
            other = {"gz": place["gz"] + by, axis: place[axis] - by}

            @pl.when(there)
            def _():
                pl.semaphore_signal(barrier, inc=1, device_id=other, device_id_type=MESH)

            greeted = greeted + jnp.where(there, 1, 0)

    for load in loads[1:]:
        load.start()

    depth, width, height = fields_ref.shape[1:]
    plane = (width, height)
    lane = iota(plane, 1)
    row = iota(plane, 0)
    levels = range(depth)

    def later_x(field):
        return [jnp.where(row == width - 1, 0.0, pltpu.roll(f, width - 1, 0)) for f in field]

    def later_y(field):
        return [jnp.where(lane == height - 1, 0.0, pltpu.roll(f, height - 1, 1)) for f in field]

    def magnetic_inside(source, stage):
        ex, ey, ez = ([source[c, z] for z in levels] for c in range(3))
        none = jnp.zeros(plane, jnp.float32)
        ey_z, ex_z = ey[1:] + [none], ex[1:] + [none]
        ey_x, ez_x = later_x(ey), later_x(ez)
        ex_y, ez_y = later_y(ex), later_y(ez)
        for z in levels:
            curl = (
                (ez_y[z] - ez[z]) - (ey_z[z] - ey[z]),
                (ex_z[z] - ex[z]) - (ez_x[z] - ez[z]),
                (ey_x[z] - ey[z]) - (ex_y[z] - ex[z]),
            )
            for c in range(3):
                inner_ref[stage, c, z] = source[3 + c, z] - COURANT * curl[c]

    def pack_faces(source, stage):
        for side, ref, edge_x, edge_y in (
            (0, source, 0, 0),
            (1, inner_ref.at[stage], width - 1, height - 1),
        ):
            for at, comp in enumerate((1, 2)):
                for z in levels:
                    k = at * depth + z
                    send_x[stage, side, k : k + 1, :] = ref[comp, z, edge_x : edge_x + 1, :]
            packed = jnp.zeros(plane, jnp.float32)
            for at, comp in enumerate((0, 2)):
                for z in levels:
                    column = ref[comp, z, :, edge_y : edge_y + 1]
                    packed = jnp.where(
                        lane == at * depth + z, jnp.broadcast_to(column, plane), packed
                    )
            send_y[stage, side] = packed

    def exchange(source, stage):
        low, high = pl.ds(0, 8), pl.ds(width - 8, 8)
        plan = (
            (source.at[pl.ds(0, 2), 0], halo_z.at[stage, 0], {"gz": -1}),
            (inner_ref.at[stage, pl.ds(0, 2), depth - 1], halo_z.at[stage, 1], {"gz": 1}),
            (source.at[2, depth - 1], edge_zy.at[stage], {"gz": 1, "gy": -1}),
            (source.at[2, depth - 1, low], edge_zx.at[stage], {"gz": 1, "gx": -1}),
            (source.at[0, 0, high], edge_xz.at[stage], {"gx": 1, "gz": -1}),
            (source.at[1, 0], edge_yz.at[stage], {"gy": 1, "gz": -1}),
            (send_x.at[stage, 0], halo_x.at[stage, 0], {"gx": -1}),
            (send_x.at[stage, 1], halo_x.at[stage, 1], {"gx": 1}),
            (send_y.at[stage, 0], halo_y.at[stage, 0], {"gy": -1}),
            (send_y.at[stage, 1], halo_y.at[stage, 1], {"gy": 1}),
            (source.at[0, :, high], edge_xy.at[stage], {"gx": 1, "gy": -1}),
            (source.at[1, :, low], edge_yx.at[stage], {"gy": 1, "gx": -1}),
        )
        out = []
        for number, (src, dst, move) in enumerate(plan):
            sends = takes = None
            for axis, by in move.items():
                last = counts[AXES.index(axis)] - 1
                up, down = place[axis] < last, place[axis] > 0
                send, take = (up, down) if by > 0 else (down, up)
                sends = send if sends is None else jnp.logical_and(sends, send)
                takes = take if takes is None else jnp.logical_and(takes, take)
            copy = pltpu.make_async_remote_copy(
                src_ref=src,
                dst_ref=dst,
                send_sem=send_sem.at[stage, number],
                recv_sem=recv_sem.at[stage, number],
                device_id={axis: place[axis] + by for axis, by in move.items()},
                device_id_type=MESH,
            )
            pl.when(sends)(copy.start)
            out.append((copy, dst, sends, takes))
        return out

    def land(copies):
        for copy, dst, sends, takes in copies:
            pl.when(takes)(copy.wait_recv)

    def spread_row(line):
        return jnp.broadcast_to(line, plane)

    def complete(source, target, stage):
        half = COURANT
        last_row, last_lane = row == width - 1, lane == height - 1
        column = [[None] * depth for _ in range(4)]
        line = [[None] * depth for _ in range(4)]
        for k in range(2):
            for z in levels:
                n = k * depth + z
                for side in range(2):
                    column[2 * side + k][z] = jnp.broadcast_to(
                        halo_y[stage, side, :, n : n + 1], plane
                    )
                    line[2 * side + k][z] = halo_x[stage, side, n : n + 1, :]
        hx, hy, hz = ([inner_ref[stage, c, z] for z in levels] for c in range(3))
        top = depth - 1
        for z in levels:
            ey_x, ez_x = spread_row(line[0][z]), spread_row(line[1][z])
            ex_y, ez_y = column[0][z], column[1][z]
            hx[z] = hx[z] - jnp.where(last_lane, half * ez_y, 0.0)
            hy[z] = hy[z] + jnp.where(last_row, half * ez_x, 0.0)
            hz[z] = hz[z] + (
                jnp.where(last_lane, half * ex_y, 0.0) - jnp.where(last_row, half * ey_x, 0.0)
            )
        hx[top] = hx[top] + half * halo_z[stage, 0, 1]
        hy[top] = hy[top] - half * halo_z[stage, 0, 0]
        for z in levels:
            target[3, z] = hx[z]
            target[4, z] = hy[z]
            target[5, z] = hz[z]
        in_z = jnp.where(at_z > 0, half, 0.0)
        in_x = jnp.where(at_x > 0, half, 0.0)
        in_y = jnp.where(at_y > 0, half, 0.0)
        first = edge_zy[stage, :, 0:1]
        hx_z = (
            halo_z[stage, 1, 0]
            + in_z * source[1, 0]
            - jnp.where(last_lane, half * jnp.broadcast_to(first, plane), 0.0)
        )
        hy_z = (
            halo_z[stage, 1, 1]
            - in_z * source[0, 0]
            + jnp.where(last_row, half * spread_row(edge_zx[stage, 0:1, :]), 0.0)
        )
        lane_row = iota((1, height), 1)
        hy_x, hz_x = [], []
        for z in levels:
            low_y = line[2][z] + in_x * source[2, z, 0:1, :]
            if z == top:
                low_y = low_y - half * edge_xz[stage, 7:8, :]
            corner = jnp.broadcast_to(edge_xy[stage, z, 7:8, 0:1], (1, height))
            low_z = (
                line[3][z]
                - in_x * source[1, z, 0:1, :]
                + jnp.where(lane_row == height - 1, half * corner, 0.0)
            )
            hy_x.append(spread_row(low_y))
            hz_x.append(spread_row(low_z))
        hx_y, hz_y = [], []
        for z in levels:
            low_x = column[2][z] - in_y * jnp.broadcast_to(source[2, z, :, 0:1], plane)
            if z == top:
                final = edge_yz[stage, :, height - 1 : height]
                low_x = low_x + half * jnp.broadcast_to(final, plane)
            corner = jnp.broadcast_to(edge_yx[stage, z, 0:1, height - 1 : height], plane)
            low_z = (
                column[3][z]
                + in_y * jnp.broadcast_to(source[0, z, :, 0:1], plane)
                - jnp.where(last_row, half * corner, 0.0)
            )
            hx_y.append(low_x)
            hz_y.append(low_z)

        def before_x(field, edge):
            return [jnp.where(row == 0, e, pltpu.roll(f, 1, 0)) for f, e in zip(field, edge)]

        def before_y(field, edge):
            return [jnp.where(lane == 0, e, pltpu.roll(f, 1, 1)) for f, e in zip(field, edge)]

        hx_z, hy_z = [hx_z] + hx[:-1], [hy_z] + hy[:-1]
        hy_x, hz_x = before_x(hy, hy_x), before_x(hz, hz_x)
        hx_y, hz_y = before_y(hx, hx_y), before_y(hz, hz_y)
        for z in levels:
            curl = (
                (hz[z] - hz_y[z]) - (hy[z] - hy_z[z]),
                (hx[z] - hx_z[z]) - (hz[z] - hz_x[z]),
                (hy[z] - hy_x[z]) - (hx[z] - hx_y[z]),
            )
            for c in range(3):
                target[c, z] = keep[z] * source[c, z] + gain[z] * curl[c]

    tile_x, tile_y = width // BLOCK, height // BLOCK
    spots = tile_x * tile_y
    freqs = wave_ref.shape[0]
    columns = 2 * freqs * dirs

    def steering(dz):
        spot = iota((1, columns), 1)
        spot_d = spot % dirs
        spot_f = (spot // dirs) % freqs
        base = (me * n_gz + wrapped(at_z, dz, n_gz)) * dirs
        polar = jnp.zeros((1, columns), jnp.float32)
        azimuth = jnp.zeros((1, columns), jnp.float32)
        wave = jnp.zeros((1, columns), jnp.float32)
        for d in range(dirs):
            polar = jnp.where(spot_d == d, angles_ref[0, base + d], polar)
            azimuth = jnp.where(spot_d == d, angles_ref[1, base + d], azimuth)
        for f in range(freqs):
            wave = jnp.where(spot_f == f, wave_ref[f], wave)
        sin_p, cos_p = sin_cos(polar)
        sin_a, cos_a = sin_cos(azimuth)
        unit_x, unit_y, unit_z = sin_p * cos_a, sin_p * sin_a, cos_p

        highs = tile_y // 8
        coarse = iota((tile_x * highs, columns), 0)
        low = iota((8, columns), 0).astype(jnp.float32)
        quarter = jnp.where(spot >= columns // 2, math.pi / 2, 0.0)
        sin_c, cos_c = sin_cos(
            wave
            * (
                unit_x * (coarse // highs).astype(jnp.float32)
                + unit_y * (coarse % highs * 8).astype(jnp.float32)
            )
            - quarter
        )
        sin_l, cos_l = sin_cos(wave * (unit_y * low))
        table = [
            cos_c[k : k + 1] * cos_l - sin_c[k : k + 1] * sin_l for k in range(tile_x * highs)
        ]
        table_ref[:, dz * columns : (dz + 1) * columns] = jnp.concatenate(table, axis=0).astype(
            jnp.bfloat16
        )
        tile = iota((in_plane, columns), 0)
        start_x = (tile // n_gy * tile_x).astype(jnp.float32)
        start_y = (tile % n_gy * tile_y).astype(jnp.float32)
        start_z = at_z.astype(jnp.float32)
        return sin_cos(wave * (unit_x * start_x + unit_y * start_y + unit_z * start_z))

    loads[0].wait()
    magnetic_inside(fields_ref, 0)
    pack_faces(fields_ref, 0)
    pl.semaphore_wait(barrier, greeted)
    first = exchange(fields_ref, 0)
    for load in loads[1:]:
        load.wait()
    material = material_ref[...]
    loss = jnp.zeros(material.shape, jnp.float32)
    eps = jnp.zeros(material.shape, jnp.float32)
    for label in range(eps_ref.shape[0]):
        chosen = material == label
        loss = jnp.where(chosen, loss_ref[label], loss)
        eps = jnp.where(chosen, eps_ref[label], eps)
    keep = (1.0 - loss) / (1.0 + loss)
    gain = COURANT / (eps * (1.0 + loss))
    order = levels_away + [0]
    shares = [order[0::4], order[1::4] + order[2::4], order[3::4]]
    turns = {dz: steering(dz) for dz in shares[0]}
    land(first)
    complete(fields_ref, mid_ref, 0)
    magnetic_inside(mid_ref, 1)
    pack_faces(mid_ref, 1)
    second = exchange(mid_ref, 1)
    masks = faces_ref[...].astype(jnp.float32)
    turns.update({dz: steering(dz) for dz in shares[1]})
    land(second)
    complete(mid_ref, state_ref, 1)

    parts = (
        (5, 0, -1.0), (4, 0, 1.0), (2, 0, 1.0), (1, 0, -1.0),
        (5, 1, 1.0), (3, 1, -1.0), (2, 1, -1.0), (0, 1, 1.0),
        (4, 2, -1.0), (3, 2, 1.0), (1, 2, 1.0), (0, 2, -1.0),
    )
    sums = []
    for comp, normal, sign in parts:
        one = state_ref[comp, 0] * masks[normal, 0]
        for z in range(1, depth):
            one = one + state_ref[comp, z] * masks[normal, z]
        sums.append(one * (sign / BLOCK**3))
    stacked = jnp.concatenate(sums, axis=0)
    take = (iota((height, spots), 1) % tile_y == iota((height, spots), 0) // BLOCK)
    spread = split_dot(stacked, take.astype(jnp.float32).astype(jnp.bfloat16))
    own = iota((width, spots), 1) // tile_y == iota((width, spots), 0) // BLOCK
    own_rows = [
        jnp.sum(
            jnp.where(own, spread[c * width : (c + 1) * width], 0.0), axis=0, keepdims=True
        )
        for c in range(CHANNELS)
    ]
    own_rows.append(jnp.zeros((ROWS - CHANNELS, spots), jnp.float32))
    gathered[me] = jnp.concatenate(own_rows, axis=0).astype(jnp.bfloat16)

    def rows_copy(slot, other, number):
        return pltpu.make_async_remote_copy(
            src_ref=gathered.at[slot],
            dst_ref=gathered.at[slot],
            send_sem=rows_send_sem.at[number],
            recv_sem=rows_recv_sem.at[slot],
            device_id=other,
            device_id_type=MESH,
        )

    each_in_plane(lambda other, number: rows_copy(me, other, number).start())
    turns.update({dz: steering(dz) for dz in shares[2]})
    each_in_plane(lambda other, number: rows_copy(number, other, number).wait_recv())

    grid = jnp.dot(
        gathered[...].reshape(in_plane * ROWS, spots),
        table_ref[...],
        preferred_element_type=jnp.float32,
    )
    half = columns // 2
    column = iota((ROWS, columns), 1)
    scale = 8.0 / math.sqrt(total * spots)

    def part(dz):
        turn_sin, turn_cos = turns[dz]
        own = grid[:, dz * columns : (dz + 1) * columns]
        by_cos = by_sin = None
        for tile in range(in_plane):
            block = own[tile * ROWS : (tile + 1) * ROWS]
            one, two = block * turn_cos[tile : tile + 1], block * turn_sin[tile : tile + 1]
            by_cos = one if by_cos is None else by_cos + one
            by_sin = two if by_sin is None else by_sin + two
        crossed = pltpu.roll(by_sin, half, 1)
        return jnp.where(column < half, by_cos - crossed, by_cos + crossed) * scale

    def part_copy(dz):
        return pltpu.make_async_remote_copy(
            src_ref=part_out.at[dz - 1],
            dst_ref=part_in.at[dz - 1],
            send_sem=part_send_sem.at[dz - 1],
            recv_sem=part_recv_sem.at[dz - 1],
            device_id={"gz": wrapped(at_z, dz, n_gz)},
            device_id_type=MESH,
        )

    for dz in levels_away:
        part_out[dz - 1] = part(dz)
        part_copy(dz).start()
    far = part(0)
    for copy, dst, sends, takes in first + second:
        pl.when(sends)(copy.wait_send)
    each_in_plane(lambda other, number: rows_copy(me, other, number).wait_send())
    for dz in levels_away:
        part_copy(dz).wait_recv()
        far = far + part_in[dz - 1]
    turned = jnp.transpose(far)
    for k in range(2 * freqs):
        far_ref[:, k * CHANNELS : (k + 1) * CHANNELS] = turned[k * dirs : (k + 1) * dirs, :CHANNELS]
    for dz in levels_away:
        part_copy(dz).wait_send()


def hand_over(*results):
    count = len(results)

    def body(*refs):
        sems = refs[2 * count]
        copies = [
            pltpu.make_async_copy(refs[k], refs[count + k], sems.at[k]) for k in range(count)
        ]
        for copy in copies:
            copy.start()
        for copy in copies:
            copy.wait()

    return pl.pallas_call(
        body,
        out_shape=tuple(jax.ShapeDtypeStruct(r.shape, r.dtype) for r in results),
        in_specs=[pl.BlockSpec(memory_space=pl.ANY)] * count,
        out_specs=(pl.BlockSpec(memory_space=pltpu.HBM),) * count,
        scratch_shapes=[pltpu.SemaphoreType.DMA((count,))],
        compiler_params=pltpu.CompilerParams(vmem_limit_bytes=1024 * 1024),
    )(*results)


def shards(counts, fields, material, faces, permittivity, losses, angles, wavenumbers):
    total = math.prod(counts)
    depth, width, height = fields.shape[1:]
    dirs = angles.shape[1] // total
    freqs = wavenumbers.shape[0]
    n_gz, n_gx, n_gy = counts
    columns = 2 * freqs * dirs
    spots = (width // BLOCK) * (height // BLOCK)
    vmem = pl.BlockSpec(memory_space=pltpu.VMEM)
    results = pl.pallas_call(
        functools.partial(kernel, counts, dirs),
        out_shape=(
            pltpu.VMEM(fields.shape, jnp.float32),
            pltpu.VMEM((dirs, 2 * freqs * CHANNELS), jnp.float32),
        ),
        in_specs=[pl.BlockSpec(memory_space=pltpu.HBM)] * 7,
        out_specs=(vmem, vmem),
        scratch_shapes=[
            pltpu.VMEM(fields.shape, jnp.float32),
            pltpu.VMEM((2, 3) + fields.shape[1:], jnp.float32),
            pltpu.VMEM(fields.shape, jnp.float32),
            pltpu.VMEM(material.shape, jnp.int32),
            pltpu.VMEM(faces.shape, jnp.int32),
            pltpu.SMEM(permittivity.shape, jnp.float32),
            pltpu.SMEM(losses.shape, jnp.float32),
            pltpu.SMEM(angles.shape, jnp.float32),
            pltpu.SMEM(wavenumbers.shape, jnp.float32),
            pltpu.VMEM((2, 2, 2 * depth, height), jnp.float32),
            pltpu.VMEM((2, 2, width, height), jnp.float32),
            pltpu.VMEM((2, 2, 2, width, height), jnp.float32),
            pltpu.VMEM((2, 2, 2 * depth, height), jnp.float32),
            pltpu.VMEM((2, 2, width, height), jnp.float32),
            pltpu.VMEM((2, width, height), jnp.float32),
            pltpu.VMEM((2, 8, height), jnp.float32),
            pltpu.VMEM((2, 8, height), jnp.float32),
            pltpu.VMEM((2, depth, 8, height), jnp.float32),
            pltpu.VMEM((2, width, height), jnp.float32),
            pltpu.VMEM((2, depth, 8, height), jnp.float32),
            pltpu.VMEM((n_gx * n_gy, ROWS, spots), jnp.bfloat16),
            pltpu.VMEM((spots, n_gz * columns), jnp.bfloat16),
            pltpu.VMEM((max(n_gz - 1, 1), ROWS, columns), jnp.float32),
            pltpu.VMEM((max(n_gz - 1, 1), ROWS, columns), jnp.float32),
            pltpu.SemaphoreType.DMA((7,)),
            pltpu.SemaphoreType.DMA((2, 12)),
            pltpu.SemaphoreType.DMA((2, 12)),
            pltpu.SemaphoreType.DMA((n_gx * n_gy,)),
            pltpu.SemaphoreType.DMA((n_gx * n_gy,)),
            pltpu.SemaphoreType.DMA((max(n_gz - 1, 1),)),
            pltpu.SemaphoreType.DMA((max(n_gz - 1, 1),)),
        ],
        compiler_params=pltpu.CompilerParams(
            collective_id=0, has_side_effects=True, vmem_limit_bytes=60 * 1024 * 1024
        ),
    )(fields, material, faces, permittivity, losses, angles, wavenumbers)
    return hand_over(*results)


def solution(mesh):
    counts = tuple(mesh.shape[axis] for axis in AXES)
    return jax.shard_map(
        functools.partial(shards, counts),
        mesh=mesh,
        in_specs=(
            P(None, "gz", "gx", "gy"),
            P("gz", "gx", "gy"),
            P(None, "gz", "gx", "gy"),
            P(),
            P(),
            P(),
            P(),
        ),
        out_specs=(P(None, "gz", "gx", "gy"), P(("gx", "gy", "gz"), None)),
        check_vma=False,
    )
```

```python
import functools
import math

import jax
import jax.numpy as jnp
from jax import lax
from jax.experimental import pallas as pl
from jax.experimental.pallas import tpu as pltpu
from jax.sharding import PartitionSpec as P

MESH = pl.DeviceIdType.MESH
COURANT = 0.5
BLOCK = 4
CHANNELS = 12
ROWS = 16
AXES = ("gz", "gx", "gy")


def iota(shape, axis):
    return lax.broadcasted_iota(jnp.int32, shape, axis)


def split_dot(left, right):
    high = left.astype(jnp.bfloat16)
    low = (left - high.astype(jnp.float32)).astype(jnp.bfloat16)
    return jnp.dot(high, right, preferred_element_type=jnp.float32) + jnp.dot(
        low, right, preferred_element_type=jnp.float32
    )


def sin_cos(angle):
    turns = jnp.floor(angle * (2 / math.pi) + 0.5)
    rest = angle - turns * 1.5703125
    rest = rest - turns * 4.837512969970703125e-4
    rest = rest - turns * 7.54978995489188216e-8
    square = rest * rest
    sine = -1.9515295891e-4 * square + 8.3321608736e-3
    sine = (sine * square - 1.6666654611e-1) * square * rest + rest
    cosine = 2.443315711809948e-5 * square - 1.388731625493765e-3
    cosine = (cosine * square + 4.166664568298827e-2) * square * square - 0.5 * square + 1.0
    quarter = turns.astype(jnp.int32)
    odd = (quarter & 1) == 1
    sin_out = jnp.where(odd, cosine, sine)
    cos_out = jnp.where(odd, sine, cosine)
    sin_out = jnp.where((quarter & 2) == 2, -sin_out, sin_out)
    cos_out = jnp.where(((quarter + 1) & 2) == 2, -cos_out, cos_out)
    return sin_out, cos_out


def kernel(
    counts,
    dirs,
    fields_hbm,
    material_hbm,
    faces_hbm,
    eps_hbm,
    loss_hbm,
    angles_hbm,
    wave_hbm,
    state_ref,
    far_ref,
    mid_ref,
    inner_ref,
    fields_ref,
    material_ref,
    faces_ref,
    eps_ref,
    loss_ref,
    angles_ref,
    wave_ref,
    send_x,
    send_y,
    halo_z,
    halo_x,
    halo_y,
    edge_zy,
    edge_zx,
    edge_xz,
    edge_xy,
    edge_yz,
    edge_yx,
    gathered,
    table_ref,
    part_out,
    part_in,
    local_sem,
    send_sem,
    recv_sem,
    rows_send_sem,
    rows_recv_sem,
    part_send_sem,
    part_recv_sem,
):
    n_gz, n_gx, n_gy = counts
    total = n_gz * n_gx * n_gy
    place = {axis: lax.axis_index(axis) for axis in AXES}
    at_z, at_x, at_y = (place[axis] for axis in AXES)
    me = at_x * n_gy + at_y
    in_plane = n_gx * n_gy

    def wrapped(at, by, count):
        moved = at + by
        return jnp.where(moved >= count, moved - count, moved)

    def each_in_plane(act):
        for dx in range(n_gx):
            for dy in range(n_gy):
                if dx or dy:
                    other_x, other_y = wrapped(at_x, dx, n_gx), wrapped(at_y, dy, n_gy)
                    act({"gx": other_x, "gy": other_y}, other_x * n_gy + other_y)

    levels_away = sorted(range(1, n_gz), key=lambda dz: abs(2 * dz - n_gz))

    pairs = (
        (fields_hbm, fields_ref),
        (material_hbm, material_ref),
        (loss_hbm, loss_ref),
        (eps_hbm, eps_ref),
        (angles_hbm, angles_ref),
        (wave_hbm, wave_ref),
        (faces_hbm, faces_ref),
    )
    loads = [pltpu.make_async_copy(a, b, local_sem.at[k]) for k, (a, b) in enumerate(pairs)]
    loads[0].start()

    halos = (halo_z, halo_x, halo_y, edge_zy, edge_zx, edge_xz, edge_xy, edge_yz, edge_yx)
    for halo in halos:
        halo[...] = jnp.zeros(halo.shape, jnp.float32)

    barrier = pltpu.get_barrier_semaphore()
    each_in_plane(
        lambda other, number: pl.semaphore_signal(
            barrier, inc=1, device_id=other, device_id_type=MESH
        )
    )
    for dz in levels_away:
        pl.semaphore_signal(
            barrier, inc=1, device_id={"gz": wrapped(at_z, dz, n_gz)}, device_id_type=MESH
        )
    greeted = n_gx * n_gy + n_gz - 2
    for axis, last in (("gx", n_gx - 1), ("gy", n_gy - 1)):
        for by in (-1, 1):
            there = jnp.logical_and(
                place["gz"] < n_gz - 1 if by > 0 else place["gz"] > 0,
                place[axis] > 0 if by > 0 else place[axis] < last,
            )
            other = {"gz": place["gz"] + by, axis: place[axis] - by}

            @pl.when(there)
            def _():
                pl.semaphore_signal(barrier, inc=1, device_id=other, device_id_type=MESH)

            greeted = greeted + jnp.where(there, 1, 0)

    for load in loads[1:]:
        load.start()

    depth, width, height = fields_ref.shape[1:]
    plane = (width, height)
    lane = iota(plane, 1)
    row = iota(plane, 0)
    levels = range(depth)

    def later_x(field):
        return [jnp.where(row == width - 1, 0.0, pltpu.roll(f, width - 1, 0)) for f in field]

    def later_y(field):
        return [jnp.where(lane == height - 1, 0.0, pltpu.roll(f, height - 1, 1)) for f in field]

    def magnetic_inside(source, stage):
        ex, ey, ez = ([source[c, z] for z in levels] for c in range(3))
        none = jnp.zeros(plane, jnp.float32)
        ey_z, ex_z = ey[1:] + [none], ex[1:] + [none]
        ey_x, ez_x = later_x(ey), later_x(ez)
        ex_y, ez_y = later_y(ex), later_y(ez)
        for z in levels:
            curl = (
                (ez_y[z] - ez[z]) - (ey_z[z] - ey[z]),
                (ex_z[z] - ex[z]) - (ez_x[z] - ez[z]),
                (ey_x[z] - ey[z]) - (ex_y[z] - ex[z]),
            )
            for c in range(3):
                inner_ref[stage, c, z] = source[3 + c, z] - COURANT * curl[c]

    def pack_faces(source, stage, sides):
        for side, ref, edge_x, edge_y in (
            (0, source, 0, 0),
            (1, inner_ref.at[stage], width - 1, height - 1),
        ):
            if side not in sides:
                continue
            for at, comp in enumerate((1, 2)):
                for z in levels:
                    k = at * depth + z
                    send_x[stage, side, k : k + 1, :] = ref[comp, z, edge_x : edge_x + 1, :]
            packed = jnp.zeros(plane, jnp.float32)
            for at, comp in enumerate((0, 2)):
                for z in levels:
                    column = ref[comp, z, :, edge_y : edge_y + 1]
                    packed = jnp.where(
                        lane == at * depth + z, jnp.broadcast_to(column, plane), packed
                    )
            send_y[stage, side] = packed

    def exchange(source, stage, sides):
        low, high = pl.ds(0, 8), pl.ds(width - 8, 8)
        plan = (
            (source.at[pl.ds(0, 2), 0], halo_z.at[stage, 0], {"gz": -1}),
            (inner_ref.at[stage, pl.ds(0, 2), depth - 1], halo_z.at[stage, 1], {"gz": 1}),
            (source.at[2, depth - 1], edge_zy.at[stage], {"gz": 1, "gy": -1}),
            (source.at[2, depth - 1, low], edge_zx.at[stage], {"gz": 1, "gx": -1}),
            (source.at[0, 0, high], edge_xz.at[stage], {"gx": 1, "gz": -1}),
            (source.at[1, 0], edge_yz.at[stage], {"gy": 1, "gz": -1}),
            (send_x.at[stage, 0], halo_x.at[stage, 0], {"gx": -1}),
            (send_x.at[stage, 1], halo_x.at[stage, 1], {"gx": 1}),
            (send_y.at[stage, 0], halo_y.at[stage, 0], {"gy": -1}),
            (send_y.at[stage, 1], halo_y.at[stage, 1], {"gy": 1}),
            (source.at[0, :, high], edge_xy.at[stage], {"gx": 1, "gy": -1}),
            (source.at[1, :, low], edge_yx.at[stage], {"gy": 1, "gx": -1}),
        )
        out = []
        for number, (src, dst, move) in enumerate(plan):
            if (1 if number in (1, 7, 9) else 0) not in sides:
                continue
            sends = takes = None
            for axis, by in move.items():
                last = counts[AXES.index(axis)] - 1
                up, down = place[axis] < last, place[axis] > 0
                send, take = (up, down) if by > 0 else (down, up)
                sends = send if sends is None else jnp.logical_and(sends, send)
                takes = take if takes is None else jnp.logical_and(takes, take)
            copy = pltpu.make_async_remote_copy(
                src_ref=src,
                dst_ref=dst,
                send_sem=send_sem.at[stage, number],
                recv_sem=recv_sem.at[stage, number],
                device_id={axis: place[axis] + by for axis, by in move.items()},
                device_id_type=MESH,
            )
            pl.when(sends)(copy.start)
            out.append((copy, dst, sends, takes))
        return out

    def land(copies):
        for copy, dst, sends, takes in copies:
            pl.when(takes)(copy.wait_recv)

    def spread_row(line):
        return jnp.broadcast_to(line, plane)

    def complete(source, target, stage):
        half = COURANT
        last_row, last_lane = row == width - 1, lane == height - 1
        column = [[None] * depth for _ in range(4)]
        line = [[None] * depth for _ in range(4)]
        for k in range(2):
            for z in levels:
                n = k * depth + z
                for side in range(2):
                    column[2 * side + k][z] = jnp.broadcast_to(
                        halo_y[stage, side, :, n : n + 1], plane
                    )
                    line[2 * side + k][z] = halo_x[stage, side, n : n + 1, :]
        hx, hy, hz = ([inner_ref[stage, c, z] for z in levels] for c in range(3))
        top = depth - 1
        for z in levels:
            ey_x, ez_x = spread_row(line[0][z]), spread_row(line[1][z])
            ex_y, ez_y = column[0][z], column[1][z]
            hx[z] = hx[z] - jnp.where(last_lane, half * ez_y, 0.0)
            hy[z] = hy[z] + jnp.where(last_row, half * ez_x, 0.0)
            hz[z] = hz[z] + (
                jnp.where(last_lane, half * ex_y, 0.0) - jnp.where(last_row, half * ey_x, 0.0)
            )
        hx[top] = hx[top] + half * halo_z[stage, 0, 1]
        hy[top] = hy[top] - half * halo_z[stage, 0, 0]
        for z in levels:
            target[3, z] = hx[z]
            target[4, z] = hy[z]
            target[5, z] = hz[z]
        in_z = jnp.where(at_z > 0, half, 0.0)
        in_x = jnp.where(at_x > 0, half, 0.0)
        in_y = jnp.where(at_y > 0, half, 0.0)
        first = edge_zy[stage, :, 0:1]
        hx_z = (
            halo_z[stage, 1, 0]
            + in_z * source[1, 0]
            - jnp.where(last_lane, half * jnp.broadcast_to(first, plane), 0.0)
        )
        hy_z = (
            halo_z[stage, 1, 1]
            - in_z * source[0, 0]
            + jnp.where(last_row, half * spread_row(edge_zx[stage, 0:1, :]), 0.0)
        )
        lane_row = iota((1, height), 1)
        hy_x, hz_x = [], []
        for z in levels:
            low_y = line[2][z] + in_x * source[2, z, 0:1, :]
            if z == top:
                low_y = low_y - half * edge_xz[stage, 7:8, :]
            corner = jnp.broadcast_to(edge_xy[stage, z, 7:8, 0:1], (1, height))
            low_z = (
                line[3][z]
                - in_x * source[1, z, 0:1, :]
                + jnp.where(lane_row == height - 1, half * corner, 0.0)
            )
            hy_x.append(spread_row(low_y))
            hz_x.append(spread_row(low_z))
        hx_y, hz_y = [], []
        for z in levels:
            low_x = column[2][z] - in_y * jnp.broadcast_to(source[2, z, :, 0:1], plane)
            if z == top:
                final = edge_yz[stage, :, height - 1 : height]
                low_x = low_x + half * jnp.broadcast_to(final, plane)
            corner = jnp.broadcast_to(edge_yx[stage, z, 0:1, height - 1 : height], plane)
            low_z = (
                column[3][z]
                + in_y * jnp.broadcast_to(source[0, z, :, 0:1], plane)
                - jnp.where(last_row, half * corner, 0.0)
            )
            hx_y.append(low_x)
            hz_y.append(low_z)

        def before_x(field, edge):
            return [jnp.where(row == 0, e, pltpu.roll(f, 1, 0)) for f, e in zip(field, edge)]

        def before_y(field, edge):
            return [jnp.where(lane == 0, e, pltpu.roll(f, 1, 1)) for f, e in zip(field, edge)]

        hx_z, hy_z = [hx_z] + hx[:-1], [hy_z] + hy[:-1]
        hy_x, hz_x = before_x(hy, hy_x), before_x(hz, hz_x)
        hx_y, hz_y = before_y(hx, hx_y), before_y(hz, hz_y)
        for z in levels:
            curl = (
                (hz[z] - hz_y[z]) - (hy[z] - hy_z[z]),
                (hx[z] - hx_z[z]) - (hz[z] - hz_x[z]),
                (hy[z] - hy_x[z]) - (hx[z] - hx_y[z]),
            )
            for c in range(3):
                target[c, z] = keep[z] * source[c, z] + gain[z] * curl[c]

    tile_x, tile_y = width // BLOCK, height // BLOCK
    spots = tile_x * tile_y
    freqs = wave_ref.shape[0]
    columns = 2 * freqs * dirs

    def steering(dz):
        spot = iota((1, columns), 1)
        spot_d = spot % dirs
        spot_f = (spot // dirs) % freqs
        base = (me * n_gz + wrapped(at_z, dz, n_gz)) * dirs
        polar = jnp.zeros((1, columns), jnp.float32)
        azimuth = jnp.zeros((1, columns), jnp.float32)
        wave = jnp.zeros((1, columns), jnp.float32)
        for d in range(dirs):
            polar = jnp.where(spot_d == d, angles_ref[0, base + d], polar)
            azimuth = jnp.where(spot_d == d, angles_ref[1, base + d], azimuth)
        for f in range(freqs):
            wave = jnp.where(spot_f == f, wave_ref[f], wave)
        sin_p, cos_p = sin_cos(polar)
        sin_a, cos_a = sin_cos(azimuth)
        unit_x, unit_y, unit_z = sin_p * cos_a, sin_p * sin_a, cos_p

        highs = tile_y // 8
        coarse = iota((tile_x * highs, columns), 0)
        low = iota((8, columns), 0).astype(jnp.float32)
        quarter = jnp.where(spot >= columns // 2, math.pi / 2, 0.0)
        sin_c, cos_c = sin_cos(
            wave
            * (
                unit_x * (coarse // highs).astype(jnp.float32)
                + unit_y * (coarse % highs * 8).astype(jnp.float32)
            )
            - quarter
        )
        sin_l, cos_l = sin_cos(wave * (unit_y * low))
        table = [
            cos_c[k : k + 1] * cos_l - sin_c[k : k + 1] * sin_l for k in range(tile_x * highs)
        ]
        table_ref[:, dz * columns : (dz + 1) * columns] = jnp.concatenate(table, axis=0).astype(
            jnp.bfloat16
        )
        tile = iota((in_plane, columns), 0)
        start_x = (tile // n_gy * tile_x).astype(jnp.float32)
        start_y = (tile % n_gy * tile_y).astype(jnp.float32)
        start_z = at_z.astype(jnp.float32)
        return sin_cos(wave * (unit_x * start_x + unit_y * start_y + unit_z * start_z))

    loads[0].wait()
    magnetic_inside(fields_ref, 0)
    pack_faces(fields_ref, 0, (0, 1))
    pl.semaphore_wait(barrier, greeted)
    first = exchange(fields_ref, 0, (0, 1))
    for load in loads[1:]:
        load.wait()
    material = material_ref[...]
    loss = jnp.zeros(material.shape, jnp.float32)
    eps = jnp.zeros(material.shape, jnp.float32)
    for label in range(eps_ref.shape[0]):
        chosen = material == label
        loss = jnp.where(chosen, loss_ref[label], loss)
        eps = jnp.where(chosen, eps_ref[label], eps)
    keep = (1.0 - loss) / (1.0 + loss)
    gain = COURANT / (eps * (1.0 + loss))
    order = levels_away + [0]
    shares = [order[0::4], order[1::4] + order[2::4], order[3::4]]
    turns = {dz: steering(dz) for dz in shares[0]}
    land(first)
    complete(fields_ref, mid_ref, 0)
    pack_faces(mid_ref, 1, (0,))
    second = exchange(mid_ref, 1, (0,))
    magnetic_inside(mid_ref, 1)
    pack_faces(mid_ref, 1, (1,))
    second = second + exchange(mid_ref, 1, (1,))
    masks = faces_ref[...].astype(jnp.float32)
    turns.update({dz: steering(dz) for dz in shares[1]})
    land(second)
    complete(mid_ref, state_ref, 1)

    parts = (
        (5, 0, -1.0), (4, 0, 1.0), (2, 0, 1.0), (1, 0, -1.0),
        (5, 1, 1.0), (3, 1, -1.0), (2, 1, -1.0), (0, 1, 1.0),
        (4, 2, -1.0), (3, 2, 1.0), (1, 2, 1.0), (0, 2, -1.0),
    )
    sums = []
    for comp, normal, sign in parts:
        one = state_ref[comp, 0] * masks[normal, 0]
        for z in range(1, depth):
            one = one + state_ref[comp, z] * masks[normal, z]
        sums.append(one * (sign / BLOCK**3))
    stacked = jnp.concatenate(sums, axis=0)
    take = (iota((height, spots), 1) % tile_y == iota((height, spots), 0) // BLOCK)
    spread = split_dot(stacked, take.astype(jnp.float32).astype(jnp.bfloat16))
    own = iota((width, spots), 1) // tile_y == iota((width, spots), 0) // BLOCK
    own_rows = [
        jnp.sum(
            jnp.where(own, spread[c * width : (c + 1) * width], 0.0), axis=0, keepdims=True
        )
        for c in range(CHANNELS)
    ]
    own_rows.append(jnp.zeros((ROWS - CHANNELS, spots), jnp.float32))
    gathered[me] = jnp.concatenate(own_rows, axis=0).astype(jnp.bfloat16)

    def rows_copy(slot, other, number):
        return pltpu.make_async_remote_copy(
            src_ref=gathered.at[slot],
            dst_ref=gathered.at[slot],
            send_sem=rows_send_sem.at[number],
            recv_sem=rows_recv_sem.at[slot],
            device_id=other,
            device_id_type=MESH,
        )

    each_in_plane(lambda other, number: rows_copy(me, other, number).start())
    turns.update({dz: steering(dz) for dz in shares[2]})
    each_in_plane(lambda other, number: rows_copy(number, other, number).wait_recv())

    grid = jnp.dot(
        gathered[...].reshape(in_plane * ROWS, spots),
        table_ref[...],
        preferred_element_type=jnp.float32,
    )
    half = columns // 2
    column = iota((ROWS, columns), 1)
    scale = 8.0 / math.sqrt(total * spots)

    def part(dz):
        turn_sin, turn_cos = turns[dz]
        own = grid[:, dz * columns : (dz + 1) * columns]
        by_cos = by_sin = None
        for tile in range(in_plane):
            block = own[tile * ROWS : (tile + 1) * ROWS]
            one, two = block * turn_cos[tile : tile + 1], block * turn_sin[tile : tile + 1]
            by_cos = one if by_cos is None else by_cos + one
            by_sin = two if by_sin is None else by_sin + two
        crossed = pltpu.roll(by_sin, half, 1)
        return jnp.where(column < half, by_cos - crossed, by_cos + crossed) * scale

    def part_copy(dz):
        return pltpu.make_async_remote_copy(
            src_ref=part_out.at[dz - 1],
            dst_ref=part_in.at[dz - 1],
            send_sem=part_send_sem.at[dz - 1],
            recv_sem=part_recv_sem.at[dz - 1],
            device_id={"gz": wrapped(at_z, dz, n_gz)},
            device_id_type=MESH,
        )

    for dz in levels_away:
        part_out[dz - 1] = part(dz)
        part_copy(dz).start()
    far = part(0)
    for copy, dst, sends, takes in first + second:
        pl.when(sends)(copy.wait_send)
    each_in_plane(lambda other, number: rows_copy(me, other, number).wait_send())
    for dz in levels_away:
        part_copy(dz).wait_recv()
        far = far + part_in[dz - 1]
    turned = jnp.transpose(far)
    for k in range(2 * freqs):
        far_ref[:, k * CHANNELS : (k + 1) * CHANNELS] = turned[k * dirs : (k + 1) * dirs, :CHANNELS]
    for dz in levels_away:
        part_copy(dz).wait_send()


def hand_over(*results):
    count = len(results)

    def body(*refs):
        sems = refs[2 * count]
        copies = [
            pltpu.make_async_copy(refs[k], refs[count + k], sems.at[k]) for k in range(count)
        ]
        for copy in copies:
            copy.start()
        for copy in copies:
            copy.wait()

    return pl.pallas_call(
        body,
        out_shape=tuple(jax.ShapeDtypeStruct(r.shape, r.dtype) for r in results),
        in_specs=[pl.BlockSpec(memory_space=pl.ANY)] * count,
        out_specs=(pl.BlockSpec(memory_space=pltpu.HBM),) * count,
        scratch_shapes=[pltpu.SemaphoreType.DMA((count,))],
        compiler_params=pltpu.CompilerParams(vmem_limit_bytes=1024 * 1024),
    )(*results)


def shards(counts, fields, material, faces, permittivity, losses, angles, wavenumbers):
    total = math.prod(counts)
    depth, width, height = fields.shape[1:]
    dirs = angles.shape[1] // total
    freqs = wavenumbers.shape[0]
    n_gz, n_gx, n_gy = counts
    columns = 2 * freqs * dirs
    spots = (width // BLOCK) * (height // BLOCK)
    vmem = pl.BlockSpec(memory_space=pltpu.VMEM)
    results = pl.pallas_call(
        functools.partial(kernel, counts, dirs),
        out_shape=(
            pltpu.VMEM(fields.shape, jnp.float32),
            pltpu.VMEM((dirs, 2 * freqs * CHANNELS), jnp.float32),
        ),
        in_specs=[pl.BlockSpec(memory_space=pltpu.HBM)] * 7,
        out_specs=(vmem, vmem),
        scratch_shapes=[
            pltpu.VMEM(fields.shape, jnp.float32),
            pltpu.VMEM((2, 3) + fields.shape[1:], jnp.float32),
            pltpu.VMEM(fields.shape, jnp.float32),
            pltpu.VMEM(material.shape, jnp.int32),
            pltpu.VMEM(faces.shape, jnp.int32),
            pltpu.SMEM(permittivity.shape, jnp.float32),
            pltpu.SMEM(losses.shape, jnp.float32),
            pltpu.SMEM(angles.shape, jnp.float32),
            pltpu.SMEM(wavenumbers.shape, jnp.float32),
            pltpu.VMEM((2, 2, 2 * depth, height), jnp.float32),
            pltpu.VMEM((2, 2, width, height), jnp.float32),
            pltpu.VMEM((2, 2, 2, width, height), jnp.float32),
            pltpu.VMEM((2, 2, 2 * depth, height), jnp.float32),
            pltpu.VMEM((2, 2, width, height), jnp.float32),
            pltpu.VMEM((2, width, height), jnp.float32),
            pltpu.VMEM((2, 8, height), jnp.float32),
            pltpu.VMEM((2, 8, height), jnp.float32),
            pltpu.VMEM((2, depth, 8, height), jnp.float32),
            pltpu.VMEM((2, width, height), jnp.float32),
            pltpu.VMEM((2, depth, 8, height), jnp.float32),
            pltpu.VMEM((n_gx * n_gy, ROWS, spots), jnp.bfloat16),
            pltpu.VMEM((spots, n_gz * columns), jnp.bfloat16),
            pltpu.VMEM((max(n_gz - 1, 1), ROWS, columns), jnp.float32),
            pltpu.VMEM((max(n_gz - 1, 1), ROWS, columns), jnp.float32),
            pltpu.SemaphoreType.DMA((7,)),
            pltpu.SemaphoreType.DMA((2, 12)),
            pltpu.SemaphoreType.DMA((2, 12)),
            pltpu.SemaphoreType.DMA((n_gx * n_gy,)),
            pltpu.SemaphoreType.DMA((n_gx * n_gy,)),
            pltpu.SemaphoreType.DMA((max(n_gz - 1, 1),)),
            pltpu.SemaphoreType.DMA((max(n_gz - 1, 1),)),
        ],
        compiler_params=pltpu.CompilerParams(
            collective_id=0, has_side_effects=True, vmem_limit_bytes=60 * 1024 * 1024
        ),
    )(fields, material, faces, permittivity, losses, angles, wavenumbers)
    return hand_over(*results)


def solution(mesh):
    counts = tuple(mesh.shape[axis] for axis in AXES)
    return jax.shard_map(
        functools.partial(shards, counts),
        mesh=mesh,
        in_specs=(
            P(None, "gz", "gx", "gy"),
            P("gz", "gx", "gy"),
            P(None, "gz", "gx", "gy"),
            P(),
            P(),
            P(),
            P(),
        ),
        out_specs=(P(None, "gz", "gx", "gy"), P(("gx", "gy", "gz"), None)),
        check_vma=False,
    )
```
